32 devices in a mesh: section: 4 (over y, x), expert: 8 (over z, core).
Axes of the slice: x: 2, y: 2, z: 4, core: 2. Of those that a mesh axis runs over, the one named last changes fastest.
Arguments:
- fwd_act: bfloat16 [4, 32, 3584], P('section', 'expert'), may hold values from -6 to 6
- fwd_enter: bfloat16 [32, 3584], P('expert'), may hold values from -6 to 6
- bwd_grad: bfloat16 [4, 32, 3584], P('section', 'expert'), may hold values from -6 to 6
- bwd_enter: bfloat16 [32, 3584], P('expert'), may hold values from -6 to 6
- w_in: bfloat16 [4, 8, 3584, 2048], P('section', 'expert'), may hold values from -0.09375 to 0.09375
- w_out: bfloat16 [4, 8, 1024, 3584], P('section', 'expert'), may hold values from -0.1875 to 0.1875
- fwd_route: int32 [2, 4, 32, 2], P(None, 'section', 'expert'), may hold values from 0 to 7, all different within a row; in each aligned block of 4 rows (0 to 3, 4 to 7, ..., all dimensions but the last counted through in order) at most 2 rows name the same one
- fwd_gate: float32 [2, 4, 32, 2], P(None, 'section', 'expert'), may hold values from 0.2 to 2
- bwd_route: int32 [2, 4, 32, 2], P(None, 'section', 'expert'), may hold values from 0 to 7, all different within a row; in each aligned block of 4 rows (0 to 3, 4 to 7, ..., all dimensions but the last counted through in order) at most 2 rows name the same one
- bwd_gate: float32 [2, 4, 32, 2], P(None, 'section', 'expert'), may hold values from 0.2 to 2
- saved_pre: float32 [2, 4, 8, 16, 2048], P(None, 'section', 'expert'), may hold values from -6 to 6
Outputs:
- fwd_out: bfloat16 [2, 4, 32, 3584], P(None, 'section', 'expert')
- bwd_out: bfloat16 [2, 4, 32, 3584], P(None, 'section', 'expert')
The draws below stay inside these ranges and needn't reach their ends.
Inputs may be any that keep to these rules, and one draw needn't show every extreme that they name: `fwd_route`: each token names 2 different experts. Within the 4 tokens of one index of expert at one tick and section, no expert is named by more than 2 routes, and some such block reaches 2. `bwd_route`: as for fwd_route.
All inputs are finite; a program needn't handle non-finite values.
Results may differ from the reference program's by a relative error of at most 0.019.
Values may be sent and summed in bfloat16 or wider, within the bound.
No kernel may reach another device: no remote copies, remote signals or barrier semaphores. Data moves between devices by JAX's collectives and lax.ppermute only.
A program may use at most 64 MiB of HBM per device.

```python
import math
import jax
import jax.numpy as jnp
import numpy as np
from jax import lax

D = 3584
FF = 1024
SLICES = 1
TOP = 2
TICKS = 2
TOK_DEV = 4
EXPERTS = 8
MOST = 2
HID = 1024
SLOTS = 16
TOKENS = 32
SECTIONS = 4
N_EXPERT = 8


def levels(stream_key, dims, cuts, smallest, top_value):
    factor_of = 1.0
    for position, parts in cuts:
        draws = jax.random.uniform(jax.random.fold_in(jax.random.fold_in(stream_key, 6), position), (parts,), jnp.float32, smallest / len(cuts), top_value / len(cuts))
        factor_of = factor_of * jnp.repeat(jnp.exp(draws), dims[position] // parts).reshape((-1,) + (1,) * (len(dims) - 1 - position))
    return factor_of


def shared_out(own_key, own, number, rows, count, top, most, lean):
    order = jax.random.permutation(own_key, count)
    crowded, usual = portions_of(count, rows * top, most, lean, True), portions_of(count, rows * top, most, lean, False)
    places = jnp.arange(count)

    def named(lengths, rotation):
        used = int((lengths > 0).sum())
        fixed = max(1, used // 4)
        shifted = fixed + (places - fixed + rotation * (used - fixed)) % max(1, count - fixed)
        return jnp.zeros((count,), jnp.int32).at[order[jnp.where(places < fixed, places, shifted)]].set(jnp.asarray(lengths, jnp.int32))

    lengths = jnp.where(number % 4 == 0, named(crowded, number // 4), named(usual, number - number // 4 - 1))
    mixed = jax.random.permutation(jax.random.fold_in(own, 3), count)
    donor, taker = mixed[0:count // 2 * 2:2], mixed[1:count // 2 * 2:2]
    room = jnp.minimum(lengths[donor] - 1, most - lengths[taker]) // 2
    room = jnp.where((donor == order[0]) | (taker == order[0]) | (lengths[taker] == 0), 0, jnp.maximum(room, 0))
    shifted = jax.random.randint(jax.random.fold_in(own, 4), (count // 2,), 0, 1 << 20) % (room + 1)
    lengths = lengths.at[donor].add(-shifted).at[taker].add(shifted)
    members = jnp.searchsorted(jnp.cumsum(lengths), jnp.arange(rows * top), side="right").astype(jnp.int32)
    table = members.reshape(top, rows).T
    table = table[jax.random.permutation(jax.random.fold_in(own, 1), rows)]
    rotation = jax.random.randint(jax.random.fold_in(own, 2), (rows, 1), 0, top)
    return jnp.take_along_axis(table, (jnp.arange(top)[None, :] + rotation) % top, axis=1)


def portions_of(amount, total, reach, skew, full):
    portions = [(1 << 20) // math.isqrt(grade ** skew) + 1 for grade in range(1, amount + 1)]
    largest = reach if full else min(reach, max(-(-total // amount), total * portions[0] // sum(portions)))
    least = 1 if total - largest >= amount - 1 else 0
    counts, surplus = [largest] + [least] * (amount - 1), total - largest - least * (amount - 1)
    while surplus > 0:
        free = [i for i in range(1, amount) if counts[i] < largest] or [i for i in range(1, amount) if counts[i] < reach]
        whole, left = sum([portions[i] for i in free]), surplus
        for i in free:
            addition = min(reach - counts[i], max(1, left * portions[i] // whole), surplus)
            counts[i] = counts[i] + addition
            surplus = surplus - addition
    return np.array(counts)


def noise(key, shape, width, bound, shards=(), held_as=jnp.bfloat16):
    factor_of = levels(key, shape, shards, -0.22, 0.18) if shards else 1.0
    entries = jax.random.normal(key, shape, jnp.float32) * width * factor_of
    return jnp.minimum(jnp.maximum(entries, -bound), bound).astype(held_as)


def setup_inputs(seed: int = 0) -> dict:
    key_of = jax.random.split(jax.random.key(seed), 12)
    fwd_act = noise(key_of[0], (SECTIONS, TOKENS, D), 1.0, 6.0, ((0, 4), (1, 8)))
    fwd_enter = noise(key_of[1], (TOKENS, D), 1.0, 6.0, ((0, 8),))
    bwd_grad = noise(key_of[2], (SECTIONS, TOKENS, D), 1.0, 6.0, ((0, 4), (1, 8)))
    bwd_enter = noise(key_of[3], (TOKENS, D), 1.0, 6.0, ((0, 8),))
    w_in = noise(key_of[4], (SECTIONS, N_EXPERT, D, 2 * HID), D ** -0.5, 0.09375, ((0, 4), (1, 8)))
    w_out = noise(key_of[5], (SECTIONS, N_EXPERT, HID, D), FF ** -0.5, 0.1875, ((0, 4), (1, 8)))
    fwd_route_keys = jax.random.split(jax.random.fold_in(key_of[6], 1), TICKS * SECTIONS * TOKENS // TOK_DEV)
    fwd_route_turns = jax.random.permutation(jax.random.fold_in(key_of[6], 3), TICKS * SECTIONS * TOKENS // TOK_DEV)
    fwd_route = jax.vmap(lambda own, number: shared_out(jax.random.fold_in(key_of[6], 2), own, number, TOK_DEV, EXPERTS, TOP, MOST, 1))(fwd_route_keys, fwd_route_turns).reshape((TICKS, SECTIONS, TOKENS, TOP))
    fwd_gate = jnp.clip(jnp.exp(math.log(2.0) - 2.3025851 * jax.random.uniform(key_of[7], (TICKS, SECTIONS, TOKENS, TOP), jnp.float32) ** levels(key_of[7], (TICKS, SECTIONS, TOKENS, TOP), ((1, 4), (2, 8)), -0.2, 0.2)), 0.2, 2.0)
    bwd_route_keys = jax.random.split(jax.random.fold_in(key_of[8], 1), TICKS * SECTIONS * TOKENS // TOK_DEV)
    bwd_route_turns = jax.random.permutation(jax.random.fold_in(key_of[8], 3), TICKS * SECTIONS * TOKENS // TOK_DEV)
    bwd_route = jax.vmap(lambda own, number: shared_out(jax.random.fold_in(key_of[8], 2), own, number, TOK_DEV, EXPERTS, TOP, MOST, 1))(bwd_route_keys, bwd_route_turns).reshape((TICKS, SECTIONS, TOKENS, TOP))
    bwd_gate = jnp.clip(jnp.exp(math.log(2.0) - 2.3025851 * jax.random.uniform(key_of[9], (TICKS, SECTIONS, TOKENS, TOP), jnp.float32) ** levels(key_of[9], (TICKS, SECTIONS, TOKENS, TOP), ((1, 4), (2, 8)), -0.2, 0.2)), 0.2, 2.0)
    saved_pre = noise(key_of[10], (TICKS, SECTIONS, N_EXPERT, SLOTS, 2 * HID), 1.0, 6.0, ((1, 4), (2, 8)), jnp.float32)
    return {"fwd_act": fwd_act, "fwd_enter": fwd_enter, "bwd_grad": bwd_grad, "bwd_enter": bwd_enter, "w_in": w_in, "w_out": w_out, "fwd_route": fwd_route, "fwd_gate": fwd_gate, "bwd_route": bwd_route, "bwd_gate": bwd_gate, "saved_pre": saved_pre}


def route_tables(routing, weights):
    route_total = TOK_DEV * TOP
    flat_route = routing.reshape(N_EXPERT, route_total)
    flat_weight = weights.reshape(N_EXPERT, route_total).astype(jnp.float32)
    positions = jnp.arange(route_total, dtype=jnp.int32)
    same_expert = flat_route[:, :, None] == flat_route[:, None, :]
    earlier = positions[None, :] < positions[:, None]
    route_rank = jnp.sum((same_expert & earlier[None]).astype(jnp.int32), axis=2)
    slot_index = flat_route * MOST + route_rank
    slot_onehot = (slot_index[:, :, None] == jnp.arange(EXPERTS * MOST, dtype=jnp.int32)[None, None, :]).astype(jnp.float32)
    token_onehot = ((positions // TOP)[:, None] == jnp.arange(TOK_DEV, dtype=jnp.int32)[None, :]).astype(jnp.float32)
    select = jnp.einsum("plm,lt->pmt", slot_onehot, token_onehot)
    combine = jnp.einsum("plm,lt,pl->ptm", slot_onehot, token_onehot, flat_weight)
    return select, combine


def dispatch(tokens, select):
    token_grid = tokens.reshape(N_EXPERT, TOK_DEV, D).astype(jnp.float32)
    placed = jnp.einsum("pmt,ptd->pmd", select, token_grid, precision=lax.Precision.HIGHEST)
    placed = placed.reshape(N_EXPERT, EXPERTS, MOST, D).transpose(1, 0, 2, 3)
    placed = jnp.repeat(placed, SLICES, axis=0)
    return placed.reshape(N_EXPERT, SLOTS, D).astype(jnp.bfloat16)


def expert_forward(slot_rows, section_in, section_out):
    gate_up = jnp.einsum("qrd,qdh->qrh", slot_rows.astype(jnp.float32), section_in.astype(jnp.float32))
    hidden = (jax.nn.silu(gate_up[..., :HID]) * gate_up[..., HID:]).astype(jnp.bfloat16)
    return jnp.einsum("qrh,qhd->qrd", hidden.astype(jnp.float32), section_out.astype(jnp.float32)).astype(jnp.bfloat16)


def expert_backward(slot_grads, section_saved, section_in, section_out):
    hidden_grad = jnp.einsum("qrd,qhd->qrh", slot_grads.astype(jnp.float32), section_out.astype(jnp.float32))
    gate_pre = section_saved[..., :HID]
    up_pre = section_saved[..., HID:]
    sigmoid_gate = jax.nn.sigmoid(gate_pre)
    activated = gate_pre * sigmoid_gate
    silu_slope = sigmoid_gate * (1.0 + gate_pre * (1.0 - sigmoid_gate))
    joined = jnp.concatenate([hidden_grad * up_pre * silu_slope, hidden_grad * activated], axis=-1).astype(jnp.bfloat16)
    return jnp.einsum("qrh,qdh->qrd", joined.astype(jnp.float32), section_in.astype(jnp.float32)).astype(jnp.bfloat16)


def gather_back(partial_value, tokens, combine):
    summed = partial_value.reshape(EXPERTS, SLICES, N_EXPERT, MOST, D).astype(jnp.float32).sum(axis=1)
    summed = summed.transpose(1, 0, 2, 3).reshape(N_EXPERT, EXPERTS * MOST, D)
    token_grid = tokens.reshape(N_EXPERT, TOK_DEV, D).astype(jnp.float32)
    mixed = token_grid + jnp.einsum("ptm,pmd->ptd", combine, summed, precision=lax.Precision.HIGHEST)
    return mixed.reshape(TOKENS, D).astype(jnp.bfloat16)


def section_step(operands):
    fwd_tokens, fwd_routing, fwd_weights, bwd_tokens, bwd_routing, bwd_weights, section_in, section_out, section_saved = operands
    select, combine = route_tables(fwd_routing, fwd_weights)
    forward_part = expert_forward(dispatch(fwd_tokens, select), section_in, section_out)
    forward_next = gather_back(forward_part, fwd_tokens, combine)
    select, combine = route_tables(bwd_routing, bwd_weights)
    backward_part = expert_backward(dispatch(bwd_tokens, select), section_saved, section_in, section_out)
    backward_next = gather_back(backward_part, bwd_tokens, combine)
    return forward_next, backward_next


def reference(fwd_act, fwd_enter, bwd_grad, bwd_enter, w_in, w_out, fwd_route, fwd_gate, bwd_route, bwd_gate, saved_pre):
    fwd_now = fwd_act
    bwd_now = bwd_grad
    fwd_list = []
    bwd_list = []
    for tick_index in range(TICKS):
        fwd_next, bwd_next = lax.map(section_step, (fwd_now, fwd_route[tick_index], fwd_gate[tick_index], bwd_now, bwd_route[tick_index], bwd_gate[tick_index], w_in, w_out, saved_pre[tick_index]))
        fwd_list.append(fwd_next)
        bwd_list.append(bwd_next)
        fwd_now = jnp.concatenate([fwd_enter[None], fwd_next[:-1]], axis=0)
        bwd_now = jnp.concatenate([bwd_next[1:], bwd_enter[None]], axis=0)
    return jnp.stack(fwd_list), jnp.stack(bwd_list)
```

```python
import functools

import jax
import jax.numpy as jnp
from jax import lax
from jax.experimental import pallas as pl
from jax.experimental.pallas import tpu as pltpu
from jax.sharding import PartitionSpec as P

FF = 1024
TICKS = 2
LANES = 128
VMEM_LIMIT = 48 * 1024 * 1024


def pack_kernel(fwd_ref, bwd_ref, fwd_route_ref, fwd_gate_ref, bwd_route_ref, bwd_gate_ref, out_ref):
    tokens, width = fwd_ref.shape[1:]
    out_ref[:tokens, :width] = fwd_ref[0]
    out_ref[tokens:, :width] = bwd_ref[0]
    lane = lax.broadcasted_iota(jnp.int32, (tokens, LANES), 1)
    for row, (route_ref, gate_ref) in enumerate(
        ((fwd_route_ref, fwd_gate_ref), (bwd_route_ref, bwd_gate_ref))
    ):
        meta = jnp.zeros((tokens, LANES), jnp.float32)
        position = 0
        for tick in range(TICKS):
            route = route_ref[tick, 0].astype(jnp.float32)
            gate = gate_ref[tick, 0]
            high = gate.astype(jnp.bfloat16).astype(jnp.float32)
            for column in range(route.shape[1]):
                for field in (route, high, gate - high):
                    meta = jnp.where(lane == position, field[:, column : column + 1], meta)
                    position += 1
        out_ref[row * tokens : (row + 1) * tokens, width:] = meta.astype(jnp.bfloat16)


def pack(fwd_now, bwd_now, fwd_route, fwd_gate, bwd_route, bwd_gate):
    tokens, width = fwd_now.shape[1:]
    return pl.pallas_call(
        pack_kernel,
        out_shape=jax.ShapeDtypeStruct((2 * tokens, width + LANES), jnp.bfloat16),
    )(fwd_now, bwd_now, fwd_route, fwd_gate, bwd_route, bwd_gate)


def expert_kernel(
    tick, tokens, top, slots, slices, chunk,
    meta_ref, rows_ref, saved_ref, w_in_ref, w_out_ref, out_ref,
    gate_w, up_w, down_w, slot_rows, weighted, sem,
):
    total, width = out_ref.shape
    hidden_units = w_out_ref.shape[2]
    chunks = hidden_units // chunk

    def copies(index):
        at = index * chunk
        return (
            pltpu.make_async_copy(
                w_in_ref.at[0, 0, :, pl.ds(at, chunk)], gate_w.at[index], sem.at[index, 0]
            ),
            pltpu.make_async_copy(
                w_in_ref.at[0, 0, :, pl.ds(hidden_units + at, chunk)], up_w.at[index], sem.at[index, 1]
            ),
            pltpu.make_async_copy(
                w_out_ref.at[0, 0, pl.ds(at, chunk), :], down_w.at[index], sem.at[index, 2]
            ),
        )

    for index in range(chunks):
        for copy in copies(index):
            copy.start()

    expert = (lax.axis_index("expert") // slices).astype(jnp.float32)
    meta = meta_ref[...].astype(jnp.float32)
    hit = jnp.zeros((total, 1), jnp.float32)
    gate_of = jnp.zeros((total, 1), jnp.float32)
    for column in range(top):
        at = (tick * top + column) * 3
        named = meta[:, at : at + 1] == expert
        hit = jnp.where(named, 1.0, hit)
        gate_of = jnp.where(named, meta[:, at + 1 : at + 2] + meta[:, at + 2 : at + 3], gate_of)
    row = lax.broadcasted_iota(jnp.int32, (total, total), 0)
    other = lax.broadcasted_iota(jnp.int32, (total, total), 1)
    earlier = (row // tokens == other // tokens) & (other < row)
    rank = jnp.dot(
        earlier.astype(jnp.bfloat16),
        jnp.broadcast_to(hit, (total, 2 * slots)).astype(jnp.bfloat16),
        preferred_element_type=jnp.float32,
    )
    row = lax.broadcasted_iota(jnp.int32, (total, 2 * slots), 0)
    slot = lax.broadcasted_iota(jnp.int32, (total, 2 * slots), 1)
    blocks = total // (2 * tokens)
    per_block = slots // blocks
    first = (row // tokens) % 2 * slots + row // (2 * tokens) * per_block
    place = jnp.where(
        (slot == first + rank.astype(jnp.int32)) & (hit > 0.0), 1.0, 0.0
    ).astype(jnp.bfloat16)
    slot_rows[...] = lax.dot_general(
        place, rows_ref[:, :width], (((0,), (0,)), ((), ())), preferred_element_type=jnp.float32
    ).astype(jnp.bfloat16)

    forward = slot_rows[:slots]
    backward = slot_rows[slots:]
    for index in range(chunks):
        for copy in copies(index):
            copy.wait()
        gate_mat, up_mat, down_mat = gate_w[index], up_w[index], down_w[index]
        gate = jnp.dot(forward, gate_mat, preferred_element_type=jnp.float32)
        up = jnp.dot(forward, up_mat, preferred_element_type=jnp.float32)
        hidden = (gate * jax.nn.sigmoid(gate) * up).astype(jnp.bfloat16)
        grad = lax.dot_general(
            backward, down_mat, (((1,), (1,)), ((), ())), preferred_element_type=jnp.float32
        )
        gate_pre = saved_ref[tick, 0, 0, :, index * chunk : (index + 1) * chunk]
        up_pre = saved_ref[
            tick, 0, 0, :, hidden_units + index * chunk : hidden_units + (index + 1) * chunk
        ]
        sigma = jax.nn.sigmoid(gate_pre)
        slope = sigma * (1.0 + gate_pre * (1.0 - sigma))
        joined_gate = (grad * up_pre * slope).astype(jnp.bfloat16)
        joined_up = (grad * (gate_pre * sigma)).astype(jnp.bfloat16)
        forward_add = jnp.dot(hidden, down_mat, preferred_element_type=jnp.float32)
        backward_add = lax.dot_general(
            joined_gate, gate_mat, (((1,), (1,)), ((), ())), preferred_element_type=jnp.float32
        ) + lax.dot_general(
            joined_up, up_mat, (((1,), (1,)), ((), ())), preferred_element_type=jnp.float32
        )
        if index == 0:
            weighted[:slots] = forward_add
            weighted[slots:] = backward_add
        else:
            weighted[:slots] += forward_add
            weighted[slots:] += backward_add
    parts = weighted[...].astype(jnp.bfloat16)
    out_ref[...] = (
        jnp.dot(place, parts, preferred_element_type=jnp.float32) * gate_of
    ).astype(jnp.bfloat16)


def expert_step(tick, tokens, top, meta, rows, saved_pre, w_in, w_out):
    width, hidden_units = w_in.shape[2], w_out.shape[2]
    slots = saved_pre.shape[3]
    total = rows.shape[0]
    chunk = min(hidden_units, 256)
    chunks = hidden_units // chunk
    whole = pl.BlockSpec(memory_space=pltpu.VMEM)
    meta_spec = pl.BlockSpec((total, LANES), lambda i: (0, width // LANES))
    rows_spec = pl.BlockSpec((total, width), lambda i: (0, 0))
    return pl.pallas_call(
        functools.partial(expert_kernel, tick, tokens, top, slots, FF // hidden_units, chunk),
        grid=(1,),
        out_shape=jax.ShapeDtypeStruct((total, width), jnp.bfloat16),
        in_specs=[
            meta_spec,
            rows_spec,
            whole,
            pl.BlockSpec(memory_space=pl.ANY),
            pl.BlockSpec(memory_space=pl.ANY),
        ],
        out_specs=whole,
        scratch_shapes=[
            pltpu.VMEM((chunks, width, chunk), jnp.bfloat16),
            pltpu.VMEM((chunks, width, chunk), jnp.bfloat16),
            pltpu.VMEM((chunks, chunk, width), jnp.bfloat16),
            pltpu.VMEM((2 * slots, width), jnp.bfloat16),
            pltpu.VMEM((2 * slots, width), jnp.float32),
            pltpu.SemaphoreType.DMA((chunks, 3)),
        ],
        compiler_params=pltpu.CompilerParams(vmem_limit_bytes=VMEM_LIMIT),
        cost_estimate=pl.CostEstimate(
            flops=12 * slots * width * hidden_units,
            bytes_accessed=6 * width * hidden_units,
            transcendentals=0,
        ),
    )(meta, rows, saved_pre, w_in, w_out)


def shards(
    fwd_act,
    fwd_enter,
    bwd_grad,
    bwd_enter,
    w_in,
    w_out,
    fwd_route,
    fwd_gate,
    bwd_route,
    bwd_gate,
    saved_pre,
):
    tokens = fwd_enter.shape[0]
    top = fwd_route.shape[3]
    section_index = lax.axis_index("section")
    section_total = lax.axis_size("section")
    up = [(i, i + 1) for i in range(section_total - 1)]
    down = [(j, i) for i, j in up]
    packed = pack(fwd_act, bwd_grad, fwd_route, fwd_gate, bwd_route, bwd_gate)
    meta = lax.all_gather(packed, "expert", axis=0, tiled=True)
    rows = meta
    own = jnp.concatenate([fwd_act[0], bwd_grad[0]], axis=0)
    fwd_list = []
    bwd_list = []
    for tick in range(TICKS):
        partial = expert_step(tick, tokens, top, meta, rows, saved_pre, w_in, w_out)
        summed = lax.psum_scatter(partial, "expert", scatter_dimension=0, tiled=True)
        following = (own.astype(jnp.float32) + summed.astype(jnp.float32)).astype(jnp.bfloat16)
        fwd_next, bwd_next = following[:tokens], following[tokens:]
        fwd_list.append(fwd_next)
        bwd_list.append(bwd_next)
        if tick + 1 < TICKS:
            from_below = lax.ppermute(fwd_next, "section", up)
            from_above = lax.ppermute(bwd_next, "section", down)
            fwd_now = jnp.where(section_index == 0, fwd_enter, from_below)
            bwd_now = jnp.where(section_index == section_total - 1, bwd_enter, from_above)
            own = jnp.concatenate([fwd_now, bwd_now], axis=0)
            rows = lax.all_gather(own, "expert", axis=0, tiled=True)
    return (jnp.stack(fwd_list)[:, None], jnp.stack(bwd_list)[:, None])


def solution(mesh):
    placed = (
        P("section", "expert", None),
        P("expert", None),
        P("section", "expert", None),
        P("expert", None),
        P("section", "expert", None, None),
        P("section", "expert", None, None),
        P(None, "section", "expert", None),
        P(None, "section", "expert", None),
        P(None, "section", "expert", None),
        P(None, "section", "expert", None),
        P(None, "section", "expert", None, None),
    )
    return jax.shard_map(
        shards,
        mesh=mesh,
        in_specs=placed,
        out_specs=(P(None, "section", "expert", None), P(None, "section", "expert", None)),
        check_vma=False,
    )
```

```python
import functools

import jax
import jax.numpy as jnp
from jax import lax
from jax.experimental import pallas as pl
from jax.experimental.pallas import tpu as pltpu
from jax.sharding import PartitionSpec as P

FF = 1024
TICKS = 2
VMEM_LIMIT = 40 * 1024 * 1024
VMEM = pl.BlockSpec(memory_space=pltpu.VMEM)
ANY = pl.BlockSpec(memory_space=pl.ANY)


def exact_dot(one_hot, values):
    return jnp.dot(one_hot.astype(jnp.bfloat16), values, preferred_element_type=jnp.float32)


def placing(route_ref, gate_ref, tick, direction, rows, per_expert, slices):
    route = route_ref[tick, 0]
    gate = gate_ref[tick, 0]
    top, tokens = route.shape
    block = 4 * per_expert
    row = lax.broadcasted_iota(jnp.int32, (rows, tokens), 0)
    expert = row // (block * slices)
    mine = (row // per_expert) % 2 == direction
    hit = jnp.zeros((rows, tokens), jnp.float32)
    weight = jnp.zeros((rows, tokens), jnp.float32)
    for column in range(top):
        named = route[column : column + 1, :] == expert
        hit = jnp.where(named, 1.0, hit)
        weight = jnp.where(named, gate[column : column + 1, :], weight)
    lane = lax.broadcasted_iota(jnp.int32, (rows, tokens), 1)
    rank = jnp.zeros((rows, tokens), jnp.float32)
    for token in range(tokens - 1):
        rank = rank + jnp.where(lane > token, hit[:, token : token + 1], 0.0)
    place = jnp.where(
        mine & (hit > 0.0) & (rank.astype(jnp.int32) == row % per_expert), 1.0, 0.0
    )
    return place, weight * place


def half_of(rows, width, per_expert):
    row = lax.broadcasted_iota(jnp.int32, (rows, width), 0)
    return (row // (2 * per_expert)) % 2


def pack_kernel(
    tick, per_expert, slices,
    fwd_route_ref, fwd_gate_ref, bwd_route_ref, bwd_gate_ref, fwd_ref, bwd_ref, *rest,
):
    devices, block, half_width = rest[-1].shape
    out_ref = rest[-1]
    rows = devices * block
    fwd = fwd_ref[...].reshape(fwd_ref.shape[-2:])
    bwd = bwd_ref[...].reshape(bwd_ref.shape[-2:])
    if len(rest) == 3:
        section = lax.axis_index("section")
        fwd = jnp.where(section == 0, rest[0][...], fwd)
        bwd = jnp.where(section == lax.axis_size("section") - 1, rest[1][...], bwd)
    total = jnp.zeros((rows, half_width), jnp.float32)
    for direction, (route_ref, gate_ref, tokens) in enumerate(
        ((fwd_route_ref, fwd_gate_ref, fwd), (bwd_route_ref, bwd_gate_ref, bwd))
    ):
        place, _ = placing(route_ref, gate_ref, tick, direction, rows, per_expert, slices)
        side = half_of(rows, place.shape[1], per_expert)
        for half in range(2):
            total = total + exact_dot(
                jnp.where(side == half, place, 0.0),
                tokens[:, half * half_width : (half + 1) * half_width],
            )
    out_ref[...] = total.astype(jnp.bfloat16).reshape(out_ref.shape)


def pack(tick, devices, per_expert, slices, routing, fwd, bwd, *entering):
    width = fwd.shape[-1]
    return pl.pallas_call(
        functools.partial(pack_kernel, tick, per_expert, slices),
        out_shape=pltpu.VMEM((devices, 4 * per_expert, width // 2), jnp.bfloat16),
        in_specs=[VMEM] * (6 + len(entering)),
        out_specs=VMEM,
    )(*routing, fwd, bwd, *entering)


def combine_kernel(
    tick, per_expert, slices,
    fwd_route_ref, fwd_gate_ref, bwd_route_ref, bwd_gate_ref, back_ref, fwd_ref, bwd_ref, *rest,
):
    devices, block, half_width = back_ref.shape
    rows = devices * block
    fwd = fwd_ref[...].reshape(fwd_ref.shape[-2:])
    bwd = bwd_ref[...].reshape(bwd_ref.shape[-2:])
    last = len(rest) == 6
    if last:
        section = lax.axis_index("section")
        fwd = jnp.where(section == 0, rest[0][...], fwd)
        bwd = jnp.where(section == lax.axis_size("section") - 1, rest[1][...], bwd)
    back = back_ref[...].reshape(rows, half_width)
    for direction, (route_ref, gate_ref, tokens) in enumerate(
        ((fwd_route_ref, fwd_gate_ref, fwd), (bwd_route_ref, bwd_gate_ref, bwd))
    ):
        _, weight = placing(route_ref, gate_ref, tick, direction, rows, per_expert, slices)
        side = half_of(rows, weight.shape[1], per_expert)
        sides = jnp.concatenate(
            [jnp.where(side == half, weight, 0.0) for half in range(2)], axis=1
        )
        high = sides.astype(jnp.bfloat16)
        left = sides - high.astype(jnp.float32)
        middle = left.astype(jnp.bfloat16)
        low = (left - middle.astype(jnp.float32)).astype(jnp.bfloat16)
        mixed = jnp.zeros((sides.shape[1], half_width), jnp.float32)
        for term in (low, middle, high):
            mixed = mixed + lax.dot_general(
                term, back, (((0,), (0,)), ((), ())), preferred_element_type=jnp.float32
            )
        count = tokens.shape[0]
        for half in range(2):
            columns = slice(half * half_width, (half + 1) * half_width)
            value = tokens[:, columns].astype(jnp.float32) + mixed[half * count : (half + 1) * count]
            if last:
                rest[4 + direction][tick, 0, :, columns] = value.astype(jnp.bfloat16)
            else:
                rest[direction][:, columns] = value.astype(jnp.bfloat16)
        if last:
            for earlier in range(tick):
                rest[4 + direction][earlier, 0] = rest[2 + direction][...]


def combine(tick, per_expert, slices, routing, back, fwd, bwd, *others):
    tokens, width = fwd.shape[-2:]
    if others:
        out_shape = [jax.ShapeDtypeStruct((TICKS, 1, tokens, width), jnp.bfloat16)] * 2
    else:
        out_shape = [pltpu.VMEM((tokens, width), jnp.bfloat16)] * 2
    return pl.pallas_call(
        functools.partial(combine_kernel, tick, per_expert, slices),
        out_shape=out_shape,
        in_specs=[VMEM] * (7 + len(others)),
        out_specs=[VMEM] * 2,
    )(*routing, back, fwd, bwd, *others)


def expert_kernel(
    tick, in_chunk, out_chunk,
    rows_ref, saved_ref, w_in_ref, w_out_ref, out_ref,
    w_in, w_out, saved, fwd_rows, bwd_cols, joined, parts, in_sem, out_sem, saved_sem,
):
    devices, block, half_width = rows_ref.shape
    per_expert = block // 4
    slots = devices * per_expert
    width, both = w_in.shape
    hidden_units = both // 2
    rows = devices * block

    def in_copy(index):
        at = pl.ds(index * in_chunk, in_chunk)
        return pltpu.make_async_copy(w_in_ref.at[0, 0, at, :], w_in.at[at, :], in_sem.at[index])

    def out_copy(index):
        at = pl.ds(index * out_chunk, out_chunk)
        return pltpu.make_async_copy(w_out_ref.at[0, 0, at, :], w_out.at[at, :], out_sem.at[index])

    saved_copy = pltpu.make_async_copy(saved_ref.at[tick, 0, 0], saved, saved_sem)
    saved_copy.start()
    for index in range(hidden_units // out_chunk):
        out_copy(index).start()
    for index in range(width // in_chunk):
        in_copy(index).start()

    received = rows_ref[...].reshape(rows, half_width)
    slot = lax.broadcasted_iota(jnp.int32, (2 * slots, rows), 0)
    row = lax.broadcasted_iota(jnp.int32, (2 * slots, rows), 1)
    home = (slot % slots) // per_expert * block + slot // slots * per_expert + slot % per_expert
    for half in range(2):
        columns = slice(half * half_width, (half + 1) * half_width)
        pick = jnp.where(row == home + half * 2 * per_expert, 1.0, 0.0)
        picked = exact_dot(pick, received)
        fwd_rows[:, columns] = picked[:slots].astype(jnp.bfloat16)
        bwd_cols[columns, :] = picked[slots:].T.astype(jnp.bfloat16)

    saved_copy.wait()
    gate_pre = saved[:, :hidden_units]
    sigma = jax.nn.sigmoid(gate_pre)
    slope = sigma * (1.0 + gate_pre * (1.0 - sigma))
    gate_factor = (saved[:, hidden_units:] * slope).T
    up_factor = (gate_pre * sigma).T

    for index in range(hidden_units // out_chunk):
        out_copy(index).wait()
        at = slice(index * out_chunk, (index + 1) * out_chunk)
        grad = jnp.dot(w_out[at, :], bwd_cols[...], preferred_element_type=jnp.float32)
        joined[at, :] = (grad * gate_factor[at]).astype(jnp.bfloat16)
        joined[hidden_units + at.start : hidden_units + at.stop, :] = (
            grad * up_factor[at]
        ).astype(jnp.bfloat16)

    gate_up = jnp.zeros((slots, both), jnp.float32)
    for index in range(width // in_chunk):
        in_copy(index).wait()
        at = slice(index * in_chunk, (index + 1) * in_chunk)
        mat = w_in[at, :]
        gate_up = gate_up + jnp.dot(fwd_rows[:, at], mat, preferred_element_type=jnp.float32)
        part = jnp.dot(mat, joined[...], preferred_element_type=jnp.float32)
        parts[slots:, at] = part.T.astype(jnp.bfloat16)

    gate = gate_up[:, :hidden_units]
    hidden = (gate * jax.nn.sigmoid(gate) * gate_up[:, hidden_units:]).astype(jnp.bfloat16)
    for half in range(2):
        columns = slice(half * half_width, (half + 1) * half_width)
        parts[:slots, columns] = jnp.dot(
            hidden, w_out[:, columns], preferred_element_type=jnp.float32
        ).astype(jnp.bfloat16)

    row = lax.broadcasted_iota(jnp.int32, (rows, 2 * slots), 0)
    slot = lax.broadcasted_iota(jnp.int32, (rows, 2 * slots), 1)
    home = (slot % slots) // per_expert * block + slot // slots * per_expert + slot % per_expert
    total = jnp.zeros((rows, half_width), jnp.float32)
    for half in range(2):
        spread = jnp.where(row == home + half * 2 * per_expert, 1.0, 0.0)
        total = total + exact_dot(spread, parts[:, half * half_width : (half + 1) * half_width])
    out_ref[...] = total.astype(jnp.bfloat16).reshape(out_ref.shape)


def expert_step(tick, rows, saved_pre, w_in, w_out):
    width, hidden_units = w_in.shape[2], w_out.shape[2]
    slots = saved_pre.shape[3]
    in_chunk, out_chunk = width // 7, min(hidden_units, 256)
    return pl.pallas_call(
        functools.partial(expert_kernel, tick, in_chunk, out_chunk),
        out_shape=pltpu.VMEM(rows.shape, jnp.bfloat16),
        in_specs=[VMEM, ANY, ANY, ANY],
        out_specs=VMEM,
        scratch_shapes=[
            pltpu.VMEM((width, 2 * hidden_units), jnp.bfloat16),
            pltpu.VMEM((hidden_units, width), jnp.bfloat16),
            pltpu.VMEM((slots, 2 * hidden_units), jnp.float32),
            pltpu.VMEM((slots, width), jnp.bfloat16),
            pltpu.VMEM((width, slots), jnp.bfloat16),
            pltpu.VMEM((2 * hidden_units, slots), jnp.bfloat16),
            pltpu.VMEM((2 * slots, width), jnp.bfloat16),
            pltpu.SemaphoreType.DMA((width // in_chunk,)),
            pltpu.SemaphoreType.DMA((hidden_units // out_chunk,)),
            pltpu.SemaphoreType.DMA,
        ],
        compiler_params=pltpu.CompilerParams(vmem_limit_bytes=VMEM_LIMIT),
        cost_estimate=pl.CostEstimate(
            flops=12 * slots * width * hidden_units,
            bytes_accessed=6 * width * hidden_units,
            transcendentals=0,
        ),
    )(rows, saved_pre, w_in, w_out)


def exchange(array):
    return lax.all_to_all(array, "expert", split_axis=0, concat_axis=0, tiled=True)


def shards(
    fwd_act,
    fwd_enter,
    bwd_grad,
    bwd_enter,
    w_in,
    w_out,
    fwd_route,
    fwd_gate,
    bwd_route,
    bwd_gate,
    saved_pre,
):
    devices = lax.axis_size("expert")
    slices = FF // w_out.shape[2]
    per_expert = saved_pre.shape[3] // devices
    section_total = lax.axis_size("section")
    up = [(i, i + 1) for i in range(section_total - 1)]
    down = [(j, i) for i, j in up]
    routing = [
        jnp.swapaxes(table, 2, 3) for table in (fwd_route, fwd_gate, bwd_route, bwd_gate)
    ]
    fwd_now, bwd_now, entering, earlier = fwd_act, bwd_grad, (), ()
    for tick in range(TICKS):
        sent = pack(tick, devices, per_expert, slices, routing, fwd_now, bwd_now, *entering)
        parts = expert_step(tick, exchange(sent), saved_pre, w_in, w_out)
        fwd_next, bwd_next = combine(
            tick, per_expert, slices, routing, exchange(parts), fwd_now, bwd_now, *entering, *earlier
        )
        if tick + 1 < TICKS:
            earlier = (fwd_next, bwd_next)
            entering = (fwd_enter, bwd_enter)
            fwd_now = lax.ppermute(fwd_next, "section", up)
            bwd_now = lax.ppermute(bwd_next, "section", down)
    return fwd_next, bwd_next


def solution(mesh):
    placed = (
        P("section", "expert", None),
        P("expert", None),
        P("section", "expert", None),
        P("expert", None),
        P("section", "expert", None, None),
        P("section", "expert", None, None),
        P(None, "section", "expert", None),
        P(None, "section", "expert", None),
        P(None, "section", "expert", None),
        P(None, "section", "expert", None),
        P(None, "section", "expert", None, None),
    )
    return jax.shard_map(
        shards,
        mesh=mesh,
        in_specs=placed,
        out_specs=(P(None, "section", "expert", None), P(None, "section", "expert", None)),
        check_vma=False,
    )
```

```python
import functools

import jax
import jax.numpy as jnp
from jax import lax
from jax.experimental import pallas as pl
from jax.experimental.pallas import tpu as pltpu
from jax.sharding import PartitionSpec as P

FF = 1024
TICKS = 2
EXPERT_VMEM = 16 * 1024 * 1024
SMALL_VMEM = 8 * 1024 * 1024
VMEM = pl.BlockSpec(memory_space=pltpu.VMEM)
HBM = pl.BlockSpec(memory_space=pltpu.HBM)


def exact_dot(one_hot, values):
    return jnp.dot(one_hot.astype(jnp.bfloat16), values, preferred_element_type=jnp.float32)


def placing(route_ref, gate_ref, tick, direction, rows, per_expert, slices):
    route = route_ref[tick, 0]
    gate = gate_ref[tick, 0]
    top, tokens = route.shape
    block = 4 * per_expert
    row = lax.broadcasted_iota(jnp.int32, (rows, tokens), 0)
    expert = row // (block * slices)
    mine = (row // per_expert) % 2 == direction
    hit = jnp.zeros((rows, tokens), jnp.float32)
    weight = jnp.zeros((rows, tokens), jnp.float32)
    for column in range(top):
        named = route[column : column + 1, :] == expert
        hit = jnp.where(named, 1.0, hit)
        weight = jnp.where(named, gate[column : column + 1, :], weight)
    lane = lax.broadcasted_iota(jnp.int32, (rows, tokens), 1)
    rank = jnp.zeros((rows, tokens), jnp.float32)
    for token in range(tokens - 1):
        rank = rank + jnp.where(lane > token, hit[:, token : token + 1], 0.0)
    place = jnp.where(
        mine & (hit > 0.0) & (rank.astype(jnp.int32) == row % per_expert), 1.0, 0.0
    )
    return place, weight * place


def half_of(rows, width, per_expert):
    row = lax.broadcasted_iota(jnp.int32, (rows, width), 0)
    return (row // (2 * per_expert)) % 2


def pack_kernel(
    tick, per_expert, slices,
    fwd_route_ref, fwd_gate_ref, bwd_route_ref, bwd_gate_ref, fwd_ref, bwd_ref, *rest,
):
    devices, block, half_width = rest[-1].shape
    out_ref = rest[-1]
    rows = devices * block
    fwd = fwd_ref[...].reshape(fwd_ref.shape[-2:])
    bwd = bwd_ref[...].reshape(bwd_ref.shape[-2:])
    if len(rest) == 3:
        section = lax.axis_index("section")
        fwd = jnp.where(section == 0, rest[0][...], fwd)
        bwd = jnp.where(section == lax.axis_size("section") - 1, rest[1][...], bwd)
    total = jnp.zeros((rows, half_width), jnp.float32)
    for direction, (route_ref, gate_ref, tokens) in enumerate(
        ((fwd_route_ref, fwd_gate_ref, fwd), (bwd_route_ref, bwd_gate_ref, bwd))
    ):
        place, _ = placing(route_ref, gate_ref, tick, direction, rows, per_expert, slices)
        side = half_of(rows, place.shape[1], per_expert)
        for half in range(2):
            total = total + exact_dot(
                jnp.where(side == half, place, 0.0),
                tokens[:, half * half_width : (half + 1) * half_width],
            )
    out_ref[...] = total.astype(jnp.bfloat16).reshape(out_ref.shape)


def pack(tick, devices, per_expert, slices, routing, fwd, bwd, *entering):
    width = fwd.shape[-1]
    return pl.pallas_call(
        functools.partial(pack_kernel, tick, per_expert, slices),
        out_shape=pltpu.VMEM((devices, 4 * per_expert, width // 2), jnp.bfloat16),
        in_specs=[VMEM] * (6 + len(entering)),
        out_specs=VMEM,
        compiler_params=pltpu.CompilerParams(vmem_limit_bytes=SMALL_VMEM),
    )(*routing, fwd, bwd, *entering)


def combine_kernel(
    tick, per_expert, slices,
    fwd_route_ref, fwd_gate_ref, bwd_route_ref, bwd_gate_ref, back_ref, fwd_ref, bwd_ref, *rest,
):
    devices, block, half_width = back_ref.shape
    rows = devices * block
    fwd = fwd_ref[...].reshape(fwd_ref.shape[-2:])
    bwd = bwd_ref[...].reshape(bwd_ref.shape[-2:])
    last = len(rest) == 6
    if last:
        section = lax.axis_index("section")
        fwd = jnp.where(section == 0, rest[0][...], fwd)
        bwd = jnp.where(section == lax.axis_size("section") - 1, rest[1][...], bwd)
    back = back_ref[...].reshape(rows, half_width)
    for direction, (route_ref, gate_ref, tokens) in enumerate(
        ((fwd_route_ref, fwd_gate_ref, fwd), (bwd_route_ref, bwd_gate_ref, bwd))
    ):
        _, weight = placing(route_ref, gate_ref, tick, direction, rows, per_expert, slices)
        side = half_of(rows, weight.shape[1], per_expert)
        sides = jnp.concatenate(
            [jnp.where(side == half, weight, 0.0) for half in range(2)], axis=1
        )
        high = sides.astype(jnp.bfloat16)
        left = sides - high.astype(jnp.float32)
        middle = left.astype(jnp.bfloat16)
        low = (left - middle.astype(jnp.float32)).astype(jnp.bfloat16)
        mixed = jnp.zeros((sides.shape[1], half_width), jnp.float32)
        for term in (low, middle, high):
            mixed = mixed + lax.dot_general(
                term, back, (((0,), (0,)), ((), ())), preferred_element_type=jnp.float32
            )
        count = tokens.shape[0]
        for half in range(2):
            columns = slice(half * half_width, (half + 1) * half_width)
            value = tokens[:, columns].astype(jnp.float32) + mixed[half * count : (half + 1) * count]
            if last:
                rest[4 + direction][tick, 0, :, columns] = value.astype(jnp.bfloat16)
            else:
                rest[direction][:, columns] = value.astype(jnp.bfloat16)
        if last:
            for earlier in range(tick):
                rest[4 + direction][earlier, 0] = rest[2 + direction][...]


def combine(tick, per_expert, slices, routing, back, fwd, bwd, *others):
    tokens, width = fwd.shape[-2:]
    if others:
        out_shape = [jax.ShapeDtypeStruct((TICKS, 1, tokens, width), jnp.bfloat16)] * 2
    else:
        out_shape = [pltpu.VMEM((tokens, width), jnp.bfloat16)] * 2
    return pl.pallas_call(
        functools.partial(combine_kernel, tick, per_expert, slices),
        out_shape=out_shape,
        in_specs=[VMEM] * (7 + len(others)),
        out_specs=[VMEM] * 2,
        compiler_params=pltpu.CompilerParams(vmem_limit_bytes=SMALL_VMEM),
    )(*routing, back, fwd, bwd, *others)


def expert_kernel(tick, loads, in_chunk, out_chunk, rows_ref, saved_ref, *rest):
    if loads:
        w_in_hbm, w_out_hbm, out_ref, w_in, w_out = rest[:5]
    else:
        w_in, w_out, out_ref = rest[:3]
    saved, slot_rows, joined, parts, in_sem, out_sem, saved_sem = rest[-7:]
    devices, block, half_width = rows_ref.shape
    per_expert = block // 4
    slots = devices * per_expert
    width, both = w_in.shape
    hidden_units = both // 2
    rows = devices * block

    def in_copy(index):
        at = pl.ds(index * in_chunk, in_chunk)
        return pltpu.make_async_copy(w_in_hbm.at[0, 0, at, :], w_in.at[at, :], in_sem.at[index])

    def out_copy(index):
        at = pl.ds(index * out_chunk, out_chunk)
        return pltpu.make_async_copy(w_out_hbm.at[0, 0, at, :], w_out.at[at, :], out_sem.at[index])

    saved_copy = pltpu.make_async_copy(saved_ref.at[tick, 0, 0], saved, saved_sem)
    saved_copy.start()
    if loads:
        for index in range(hidden_units // out_chunk):
            out_copy(index).start()
        for index in range(width // in_chunk):
            in_copy(index).start()

    received = rows_ref[...].reshape(rows, half_width)
    slot = lax.broadcasted_iota(jnp.int32, (2 * slots, rows), 0)
    row = lax.broadcasted_iota(jnp.int32, (2 * slots, rows), 1)
    home = (slot % slots) // per_expert * block + slot // slots * per_expert + slot % per_expert
    for half in range(2):
        pick = jnp.where(row == home + half * 2 * per_expert, 1.0, 0.0)
        slot_rows[:, half * half_width : (half + 1) * half_width] = exact_dot(
            pick, received
        ).astype(jnp.bfloat16)

    saved_copy.wait()
    for index in range(hidden_units // out_chunk):
        if loads:
            out_copy(index).wait()
        start, stop = index * out_chunk, (index + 1) * out_chunk
        grad = lax.dot_general(
            slot_rows[slots:],
            w_out[start:stop, :],
            (((1,), (1,)), ((), ())),
            preferred_element_type=jnp.float32,
        )
        gate_pre = saved[:, start:stop]
        up_pre = saved[:, hidden_units + start : hidden_units + stop]
        sigma = jax.nn.sigmoid(gate_pre)
        slope = sigma * (1.0 + gate_pre * (1.0 - sigma))
        joined[:, start:stop] = (grad * up_pre * slope).astype(jnp.bfloat16)
        joined[:, hidden_units + start : hidden_units + stop] = (
            grad * (gate_pre * sigma)
        ).astype(jnp.bfloat16)

    gate_up = jnp.zeros((slots, both), jnp.float32)
    for index in range(width // in_chunk):
        if loads:
            in_copy(index).wait()
        at = slice(index * in_chunk, (index + 1) * in_chunk)
        gate_up = gate_up + jnp.dot(
            slot_rows[:slots, at], w_in[at, :], preferred_element_type=jnp.float32
        )
        parts[slots:, at] = lax.dot_general(
            joined[...],
            w_in[at, :],
            (((1,), (1,)), ((), ())),
            preferred_element_type=jnp.float32,
        ).astype(jnp.bfloat16)

    gate = gate_up[:, :hidden_units]
    hidden = (gate * jax.nn.sigmoid(gate) * gate_up[:, hidden_units:]).astype(jnp.bfloat16)
    for half in range(2):
        columns = slice(half * half_width, (half + 1) * half_width)
        parts[:slots, columns] = jnp.dot(
            hidden, w_out[:, columns], preferred_element_type=jnp.float32
        ).astype(jnp.bfloat16)

    row = lax.broadcasted_iota(jnp.int32, (rows, 2 * slots), 0)
    slot = lax.broadcasted_iota(jnp.int32, (rows, 2 * slots), 1)
    home = (slot % slots) // per_expert * block + slot // slots * per_expert + slot % per_expert
    total = jnp.zeros((rows, half_width), jnp.float32)
    for half in range(2):
        spread = jnp.where(row == home + half * 2 * per_expert, 1.0, 0.0)
        total = total + exact_dot(spread, parts[:, half * half_width : (half + 1) * half_width])
    out_ref[...] = total.astype(jnp.bfloat16).reshape(out_ref.shape)


def expert_step(tick, rows, saved_pre, w_in, w_out):
    loads = w_in.ndim == 4
    width, both = w_in.shape[-2:]
    hidden_units = both // 2
    slots = saved_pre.shape[3]
    in_chunk, out_chunk = width // 7, min(hidden_units, 256)
    out_shape = [pltpu.VMEM(rows.shape, jnp.bfloat16)]
    if loads:
        out_shape += [
            pltpu.VMEM((width, both), jnp.bfloat16),
            pltpu.VMEM((hidden_units, width), jnp.bfloat16),
        ]
    home = HBM if loads else VMEM
    pinned = [pltpu.with_memory_space_constraint(saved_pre, pltpu.HBM), w_in, w_out]
    if loads:
        pinned[1:] = [pltpu.with_memory_space_constraint(w, pltpu.HBM) for w in (w_in, w_out)]
    return pl.pallas_call(
        functools.partial(expert_kernel, tick, loads, in_chunk, out_chunk),
        out_shape=out_shape,
        in_specs=[VMEM, HBM, home, home],
        out_specs=[VMEM] * len(out_shape),
        scratch_shapes=[
            pltpu.VMEM((slots, both), jnp.float32),
            pltpu.VMEM((2 * slots, width), jnp.bfloat16),
            pltpu.VMEM((slots, both), jnp.bfloat16),
            pltpu.VMEM((2 * slots, width), jnp.bfloat16),
            pltpu.SemaphoreType.DMA((width // in_chunk,)),
            pltpu.SemaphoreType.DMA((hidden_units // out_chunk,)),
            pltpu.SemaphoreType.DMA,
        ],
        compiler_params=pltpu.CompilerParams(vmem_limit_bytes=EXPERT_VMEM),
        cost_estimate=pl.CostEstimate(
            flops=12 * slots * width * hidden_units,
            bytes_accessed=6 * width * hidden_units,
            transcendentals=0,
        ),
    )(rows, *pinned)


def exchange(array):
    return lax.all_to_all(array, "expert", split_axis=0, concat_axis=0, tiled=True)


def shards(
    fwd_act,
    fwd_enter,
    bwd_grad,
    bwd_enter,
    w_in,
    w_out,
    fwd_route,
    fwd_gate,
    bwd_route,
    bwd_gate,
    saved_pre,
):
    devices = lax.axis_size("expert")
    slices = FF // w_out.shape[2]
    per_expert = saved_pre.shape[3] // devices
    section_total = lax.axis_size("section")
    up = [(i, i + 1) for i in range(section_total - 1)]
    down = [(j, i) for i, j in up]
    routing = [
        jnp.swapaxes(table, 2, 3) for table in (fwd_route, fwd_gate, bwd_route, bwd_gate)
    ]
    fwd_now, bwd_now, entering, earlier = fwd_act, bwd_grad, (), ()
    for tick in range(TICKS):
        sent = pack(tick, devices, per_expert, slices, routing, fwd_now, bwd_now, *entering)
        parts, *kept = expert_step(tick, exchange(sent), saved_pre, w_in, w_out)
        w_in, w_out = kept or (w_in, w_out)
        fwd_next, bwd_next = combine(
            tick, per_expert, slices, routing, exchange(parts), fwd_now, bwd_now, *entering, *earlier
        )
        if tick + 1 < TICKS:
            earlier = (fwd_next, bwd_next)
            entering = (fwd_enter, bwd_enter)
            fwd_now = lax.ppermute(fwd_next, "section", up)
            bwd_now = lax.ppermute(bwd_next, "section", down)
    return fwd_next, bwd_next


def solution(mesh):
    placed = (
        P("section", "expert", None),
        P("expert", None),
        P("section", "expert", None),
        P("expert", None),
        P("section", "expert", None, None),
        P("section", "expert", None, None),
        P(None, "section", "expert", None),
        P(None, "section", "expert", None),
        P(None, "section", "expert", None),
        P(None, "section", "expert", None),
        P(None, "section", "expert", None, None),
    )
    return jax.shard_map(
        shards,
        mesh=mesh,
        in_specs=placed,
        out_specs=(P(None, "section", "expert", None), P(None, "section", "expert", None)),
        check_vma=False,
    )
```

```python
import functools

import jax
import jax.numpy as jnp
from jax import lax
from jax.experimental import pallas as pl
from jax.experimental.pallas import tpu as pltpu
from jax.sharding import PartitionSpec as P

FF = 1024
TICKS = 2
EXPERT_VMEM = 16 * 1024 * 1024
IN_FLIGHT = 2
SMALL_VMEM = 8 * 1024 * 1024
VMEM = pl.BlockSpec(memory_space=pltpu.VMEM)
HBM = pl.BlockSpec(memory_space=pltpu.HBM)


def exact_dot(one_hot, values):
    return jnp.dot(one_hot.astype(jnp.bfloat16), values, preferred_element_type=jnp.float32)


def placing(route_ref, gate_ref, tick, direction, rows, per_expert, slices):
    route = route_ref[tick, 0]
    gate = gate_ref[tick, 0]
    top, tokens = route.shape
    block = 4 * per_expert
    row = lax.broadcasted_iota(jnp.int32, (rows, tokens), 0)
    expert = row // (block * slices)
    mine = (row // per_expert) % 2 == direction
    hit = jnp.zeros((rows, tokens), jnp.float32)
    weight = jnp.zeros((rows, tokens), jnp.float32)
    for column in range(top):
        named = route[column : column + 1, :] == expert
        hit = jnp.where(named, 1.0, hit)
        weight = jnp.where(named, gate[column : column + 1, :], weight)
    lane = lax.broadcasted_iota(jnp.int32, (rows, tokens), 1)
    rank = jnp.zeros((rows, tokens), jnp.float32)
    for token in range(tokens - 1):
        rank = rank + jnp.where(lane > token, hit[:, token : token + 1], 0.0)
    place = jnp.where(
        mine & (hit > 0.0) & (rank.astype(jnp.int32) == row % per_expert), 1.0, 0.0
    )
    return place, weight * place


def half_of(rows, width, per_expert):
    row = lax.broadcasted_iota(jnp.int32, (rows, width), 0)
    return (row // (2 * per_expert)) % 2


def whole_rows(rows_ref, index):
    block = rows_ref[index]
    count = block.shape[0] // 2
    return block[:count], block[count:]


def arriving(section_ref, enter_refs):
    section, last = lax.axis_index("section"), lax.axis_size("section") - 1
    pairs = []
    for source, edge, enter_ref in (
        (section - 1, section == 0, enter_refs[0]),
        (section + 1, section == last, enter_refs[1]),
    ):
        halves = whole_rows(section_ref, jnp.clip(source, 0, last))
        half_width = halves[0].shape[1]
        pairs.append(
            [
                jnp.where(edge, enter_ref[:, half * half_width : (half + 1) * half_width], halves[half])
                for half in range(2)
            ]
        )
    return pairs


def split_rows(rows):
    half_width = rows.shape[-1] // 2
    return [rows[:, :half_width], rows[:, half_width:]]


def pack_into(out_ref, tick, per_expert, slices, tables, pairs):
    devices, block, half_width = out_ref.shape
    rows = devices * block
    total = jnp.zeros((rows, half_width), jnp.float32)
    for direction, halves in enumerate(pairs):
        place, _ = placing(
            tables[2 * direction], tables[2 * direction + 1], tick, direction, rows, per_expert, slices
        )
        side = half_of(rows, place.shape[1], per_expert)
        for half in range(2):
            total = total + exact_dot(jnp.where(side == half, place, 0.0), halves[half])
    out_ref[...] = total.astype(jnp.bfloat16).reshape(out_ref.shape)


def first_pack_kernel(tick, per_expert, slices, *refs):
    operands, out_ref, local, sem = refs[:6], refs[6], refs[7:13], refs[13]
    copies = [
        pltpu.make_async_copy(source, target, sem.at[index])
        for index, (source, target) in enumerate(zip(operands, local))
    ]
    for copy in copies:
        copy.start()
    for copy in copies:
        copy.wait()
    pairs = [split_rows(tokens_ref[0]) for tokens_ref in local[4:]]
    pack_into(out_ref, tick, per_expert, slices, local[:4], pairs)


def first_pack(tick, devices, per_expert, slices, routing, fwd, bwd):
    operands = [*routing, fwd, bwd]
    return pl.pallas_call(
        functools.partial(first_pack_kernel, tick, per_expert, slices),
        out_shape=pltpu.VMEM((devices, 4 * per_expert, fwd.shape[-1] // 2), jnp.bfloat16),
        in_specs=[HBM] * len(operands),
        out_specs=VMEM,
        scratch_shapes=[pltpu.VMEM(operand.shape, operand.dtype) for operand in operands]
        + [pltpu.SemaphoreType.DMA((len(operands),))],
        compiler_params=pltpu.CompilerParams(vmem_limit_bytes=SMALL_VMEM),
    )(*(pltpu.with_memory_space_constraint(operand, pltpu.HBM) for operand in operands))


def later_pack_kernel(tick, per_expert, slices, *refs):
    tables, section_ref, enter_refs, out_ref = refs[:4], refs[4], refs[5:7], refs[7]
    pack_into(out_ref, tick, per_expert, slices, tables, arriving(section_ref, enter_refs))


def later_pack(tick, devices, per_expert, slices, routing, arrived, *entering):
    return pl.pallas_call(
        functools.partial(later_pack_kernel, tick, per_expert, slices),
        out_shape=pltpu.VMEM((devices, 4 * per_expert, arrived.shape[-1]), jnp.bfloat16),
        in_specs=[VMEM] * 7,
        out_specs=VMEM,
        compiler_params=pltpu.CompilerParams(vmem_limit_bytes=SMALL_VMEM),
    )(*routing, arrived, *entering)


def mixed_halves(tick, per_expert, slices, tables, back_ref, pairs):
    devices, block, half_width = back_ref.shape
    rows = devices * block
    back = back_ref[...].reshape(rows, half_width)
    results = []
    for direction, halves in enumerate(pairs):
        _, weight = placing(
            tables[2 * direction], tables[2 * direction + 1], tick, direction, rows, per_expert, slices
        )
        side = half_of(rows, weight.shape[1], per_expert)
        sides = jnp.concatenate(
            [jnp.where(side == half, weight, 0.0) for half in range(2)], axis=1
        )
        high = sides.astype(jnp.bfloat16)
        left = sides - high.astype(jnp.float32)
        middle = left.astype(jnp.bfloat16)
        low = (left - middle.astype(jnp.float32)).astype(jnp.bfloat16)
        mixed = jnp.concatenate(halves, axis=0).astype(jnp.float32)
        for term in (low, middle, high):
            mixed = mixed + lax.dot_general(
                term, back, (((0,), (0,)), ((), ())), preferred_element_type=jnp.float32
            )
        results.append(mixed.astype(jnp.bfloat16))
    return results


def relay_kernel(tick, per_expert, slices, *refs):
    tables, back_ref, token_refs, section_ref, next_refs = refs[:4], refs[4], refs[5:7], refs[7], refs[8:]
    half_width = back_ref.shape[2]
    section, last = lax.axis_index("section"), lax.axis_size("section") - 1
    pairs = [split_rows(tokens_ref[0]) for tokens_ref in token_refs]
    results = mixed_halves(tick, per_expert, slices, tables, back_ref, pairs)
    section_ref[...] = jnp.zeros_like(section_ref)
    for result, next_ref in zip(results, next_refs):
        count = result.shape[0] // 2
        for half in range(2):
            next_ref[:, half * half_width : (half + 1) * half_width] = result[
                half * count : (half + 1) * count
            ]

    @pl.when(section < last)
    def _():
        section_ref[jnp.minimum(section + 1, last)] = results[0]

    @pl.when(section > 0)
    def _():
        section_ref[jnp.maximum(section - 1, 0)] = results[1]


def relay(tick, per_expert, slices, routing, back, fwd, bwd):
    tokens, width = fwd.shape[-2:]
    sections = lax.axis_size("section")
    return pl.pallas_call(
        functools.partial(relay_kernel, tick, per_expert, slices),
        out_shape=[pltpu.VMEM((sections, 2 * tokens, width // 2), jnp.bfloat16)]
        + [pltpu.VMEM((tokens, width), jnp.bfloat16)] * 2,
        in_specs=[VMEM] * 7,
        out_specs=[VMEM] * 3,
        compiler_params=pltpu.CompilerParams(vmem_limit_bytes=SMALL_VMEM),
    )(*routing, back, fwd, bwd)


def finish_kernel(tick, per_expert, slices, *refs):
    tables, back_ref, section_ref, enter_refs, earlier_refs, out_refs = (
        refs[:4], refs[4], refs[5], refs[6:8], refs[8:10], refs[10:],
    )
    half_width = back_ref.shape[2]
    pairs = arriving(section_ref, enter_refs)
    results = mixed_halves(tick, per_expert, slices, tables, back_ref, pairs)
    for result, earlier_ref, out_ref in zip(results, earlier_refs, out_refs):
        count = result.shape[0] // 2
        out_ref[0, 0] = earlier_ref[...]
        for half in range(2):
            out_ref[tick, 0, :, half * half_width : (half + 1) * half_width] = result[
                half * count : (half + 1) * count
            ]


def finish(tick, per_expert, slices, routing, back, arrived, *others):
    tokens, width = others[0].shape
    return pl.pallas_call(
        functools.partial(finish_kernel, tick, per_expert, slices),
        out_shape=[jax.ShapeDtypeStruct((TICKS, 1, tokens, width), jnp.bfloat16)] * 2,
        in_specs=[VMEM] * 10,
        out_specs=[VMEM] * 2,
        compiler_params=pltpu.CompilerParams(vmem_limit_bytes=SMALL_VMEM),
    )(*routing, back, arrived, *others)


def expert_kernel(tick, loads, in_chunk, out_chunk, rows_ref, saved_ref, *rest):
    if loads:
        w_in_hbm, w_out_hbm, out_ref, w_in, w_out = rest[:5]
    else:
        w_in, w_out, out_ref = rest[:3]
    saved, slot_rows, joined, parts, in_sem, out_sem, saved_sem = rest[-7:]
    devices, block, half_width = rows_ref.shape
    per_expert = block // 4
    slots = devices * per_expert
    width, both = w_in.shape
    hidden_units = both // 2
    rows = devices * block

    def in_copy(index):
        at = pl.ds(index * in_chunk, in_chunk)
        return pltpu.make_async_copy(w_in_hbm.at[0, 0, at, :], w_in.at[at, :], in_sem.at[index])

    def out_copy(index):
        at = pl.ds(index * out_chunk, out_chunk)
        return pltpu.make_async_copy(w_out_hbm.at[0, 0, at, :], w_out.at[at, :], out_sem.at[index])

    saved_copy = pltpu.make_async_copy(saved_ref.at[tick, 0, 0], saved, saved_sem)
    saved_copy.start()
    copies = []
    if loads:
        copies = [out_copy(index) for index in range(hidden_units // out_chunk)]
        copies += [in_copy(index) for index in range(width // in_chunk)]
    for copy in copies[:IN_FLIGHT]:
        copy.start()

    def arrive(index):
        if loads:
            copies[index].wait()
            if index + IN_FLIGHT < len(copies):
                copies[index + IN_FLIGHT].start()

    received = rows_ref[...].reshape(rows, half_width)
    slot = lax.broadcasted_iota(jnp.int32, (2 * slots, rows), 0)
    row = lax.broadcasted_iota(jnp.int32, (2 * slots, rows), 1)
    home = (slot % slots) // per_expert * block + slot // slots * per_expert + slot % per_expert
    for half in range(2):
        pick = jnp.where(row == home + half * 2 * per_expert, 1.0, 0.0)
        slot_rows[:, half * half_width : (half + 1) * half_width] = exact_dot(
            pick, received
        ).astype(jnp.bfloat16)

    saved_copy.wait()
    for index in range(hidden_units // out_chunk):
        arrive(index)
        start, stop = index * out_chunk, (index + 1) * out_chunk
        grad = lax.dot_general(
            slot_rows[slots:],
            w_out[start:stop, :],
            (((1,), (1,)), ((), ())),
            preferred_element_type=jnp.float32,
        )
        gate_pre = saved[:, start:stop]
        up_pre = saved[:, hidden_units + start : hidden_units + stop]
        sigma = jax.nn.sigmoid(gate_pre)
        slope = sigma * (1.0 + gate_pre * (1.0 - sigma))
        joined[:, start:stop] = (grad * up_pre * slope).astype(jnp.bfloat16)
        joined[:, hidden_units + start : hidden_units + stop] = (
            grad * (gate_pre * sigma)
        ).astype(jnp.bfloat16)

    gate_up = jnp.zeros((slots, both), jnp.float32)
    for index in range(width // in_chunk):
        arrive(hidden_units // out_chunk + index)
        at = slice(index * in_chunk, (index + 1) * in_chunk)
        gate_up = gate_up + jnp.dot(
            slot_rows[:slots, at], w_in[at, :], preferred_element_type=jnp.float32
        )
        parts[slots:, at] = lax.dot_general(
            joined[...],
            w_in[at, :],
            (((1,), (1,)), ((), ())),
            preferred_element_type=jnp.float32,
        ).astype(jnp.bfloat16)

    gate = gate_up[:, :hidden_units]
    hidden = (gate * jax.nn.sigmoid(gate) * gate_up[:, hidden_units:]).astype(jnp.bfloat16)
    for half in range(2):
        columns = slice(half * half_width, (half + 1) * half_width)
        parts[:slots, columns] = jnp.dot(
            hidden, w_out[:, columns], preferred_element_type=jnp.float32
        ).astype(jnp.bfloat16)

    row = lax.broadcasted_iota(jnp.int32, (rows, 2 * slots), 0)
    slot = lax.broadcasted_iota(jnp.int32, (rows, 2 * slots), 1)
    home = (slot % slots) // per_expert * block + slot // slots * per_expert + slot % per_expert
    total = jnp.zeros((rows, half_width), jnp.float32)
    for half in range(2):
        spread = jnp.where(row == home + half * 2 * per_expert, 1.0, 0.0)
        total = total + exact_dot(spread, parts[:, half * half_width : (half + 1) * half_width])
    out_ref[...] = total.astype(jnp.bfloat16).reshape(out_ref.shape)


def expert_step(tick, rows, saved_pre, w_in, w_out):
    loads = w_in.ndim == 4
    width, both = w_in.shape[-2:]
    hidden_units = both // 2
    slots = saved_pre.shape[3]
    in_chunk, out_chunk = width // 7, min(hidden_units, 256)
    out_shape = [pltpu.VMEM(rows.shape, jnp.bfloat16)]
    if loads:
        out_shape += [
            pltpu.VMEM((width, both), jnp.bfloat16),
            pltpu.VMEM((hidden_units, width), jnp.bfloat16),
        ]
    home = HBM if loads else VMEM
    pinned = [pltpu.with_memory_space_constraint(saved_pre, pltpu.HBM), w_in, w_out]
    if loads:
        pinned[1:] = [pltpu.with_memory_space_constraint(w, pltpu.HBM) for w in (w_in, w_out)]
    return pl.pallas_call(
        functools.partial(expert_kernel, tick, loads, in_chunk, out_chunk),
        out_shape=out_shape,
        in_specs=[VMEM, HBM, home, home],
        out_specs=[VMEM] * len(out_shape),
        scratch_shapes=[
            pltpu.VMEM((slots, both), jnp.float32),
            pltpu.VMEM((2 * slots, width), jnp.bfloat16),
            pltpu.VMEM((slots, both), jnp.bfloat16),
            pltpu.VMEM((2 * slots, width), jnp.bfloat16),
            pltpu.SemaphoreType.DMA((width // in_chunk,)),
            pltpu.SemaphoreType.DMA((hidden_units // out_chunk,)),
            pltpu.SemaphoreType.DMA,
        ],
        compiler_params=pltpu.CompilerParams(vmem_limit_bytes=EXPERT_VMEM),
        cost_estimate=pl.CostEstimate(
            flops=12 * slots * width * hidden_units,
            bytes_accessed=6 * width * hidden_units,
            transcendentals=0,
        ),
    )(rows, *pinned)


def exchange(array, axis):
    return lax.all_to_all(array, axis, split_axis=0, concat_axis=0, tiled=True)


def shards(
    fwd_act,
    fwd_enter,
    bwd_grad,
    bwd_enter,
    w_in,
    w_out,
    fwd_route,
    fwd_gate,
    bwd_route,
    bwd_gate,
    saved_pre,
):
    devices = lax.axis_size("expert")
    slices = FF // w_out.shape[2]
    per_expert = saved_pre.shape[3] // devices
    routing = [
        jnp.swapaxes(table, 2, 3) for table in (fwd_route, fwd_gate, bwd_route, bwd_gate)
    ]
    sent = first_pack(0, devices, per_expert, slices, routing, fwd_act, bwd_grad)
    parts, w_in, w_out = expert_step(0, exchange(sent, "expert"), saved_pre, w_in, w_out)
    moved, fwd_next, bwd_next = relay(
        0, per_expert, slices, routing, exchange(parts, "expert"), fwd_act, bwd_grad
    )
    arrived = exchange(moved, "section")
    sent = later_pack(1, devices, per_expert, slices, routing, arrived, fwd_enter, bwd_enter)
    (parts,) = expert_step(1, exchange(sent, "expert"), saved_pre, w_in, w_out)
    return finish(
        1, per_expert, slices, routing, exchange(parts, "expert"), arrived,
        fwd_enter, bwd_enter, fwd_next, bwd_next,
    )


def solution(mesh):
    placed = (
        P("section", "expert", None),
        P("expert", None),
        P("section", "expert", None),
        P("expert", None),
        P("section", "expert", None, None),
        P("section", "expert", None, None),
        P(None, "section", "expert", None),
        P(None, "section", "expert", None),
        P(None, "section", "expert", None),
        P(None, "section", "expert", None),
        P(None, "section", "expert", None, None),
    )
    return jax.shard_map(
        shards,
        mesh=mesh,
        in_specs=placed,
        out_specs=(P(None, "section", "expert", None), P(None, "section", "expert", None)),
        check_vma=False,
    )
```

```python
import functools

import jax
import jax.numpy as jnp
from jax import lax
from jax.experimental import pallas as pl
from jax.experimental.pallas import tpu as pltpu
from jax.sharding import PartitionSpec as P

FF = 1024
TICKS = 2
EXPERT_VMEM = 16 * 1024 * 1024
BESIDE = 2000
SMALL_VMEM = 8 * 1024 * 1024
VMEM = pl.BlockSpec(memory_space=pltpu.VMEM)
HBM = pl.BlockSpec(memory_space=pltpu.HBM)


def exact_dot(one_hot, values):
    return jnp.dot(one_hot.astype(jnp.bfloat16), values, preferred_element_type=jnp.float32)


def placing(route_ref, gate_ref, tick, direction, rows, per_expert, slices):
    route = route_ref[tick, 0]
    gate = gate_ref[tick, 0]
    top, tokens = route.shape
    block = 4 * per_expert
    row = lax.broadcasted_iota(jnp.int32, (rows, tokens), 0)
    expert = row // (block * slices)
    mine = (row // per_expert) % 2 == direction
    hit = jnp.zeros((rows, tokens), jnp.float32)
    weight = jnp.zeros((rows, tokens), jnp.float32)
    for column in range(top):
        named = route[column : column + 1, :] == expert
        hit = jnp.where(named, 1.0, hit)
        weight = jnp.where(named, gate[column : column + 1, :], weight)
    lane = lax.broadcasted_iota(jnp.int32, (rows, tokens), 1)
    rank = jnp.zeros((rows, tokens), jnp.float32)
    for token in range(tokens - 1):
        rank = rank + jnp.where(lane > token, hit[:, token : token + 1], 0.0)
    place = jnp.where(
        mine & (hit > 0.0) & (rank.astype(jnp.int32) == row % per_expert), 1.0, 0.0
    )
    return place, weight * place


def half_of(rows, width, per_expert):
    row = lax.broadcasted_iota(jnp.int32, (rows, width), 0)
    return (row // (2 * per_expert)) % 2


def whole_rows(rows_ref, index):
    block = rows_ref[index]
    count = block.shape[0] // 2
    return block[:count], block[count:]


def arriving(section_ref, enter_refs):
    section, last = lax.axis_index("section"), lax.axis_size("section") - 1
    pairs = []
    for source, edge, enter_ref in (
        (section - 1, section == 0, enter_refs[0]),
        (section + 1, section == last, enter_refs[1]),
    ):
        halves = whole_rows(section_ref, jnp.clip(source, 0, last))
        half_width = halves[0].shape[1]
        pairs.append(
            [
                jnp.where(edge, enter_ref[:, half * half_width : (half + 1) * half_width], halves[half])
                for half in range(2)
            ]
        )
    return pairs


def split_rows(rows):
    half_width = rows.shape[-1] // 2
    return [rows[:, :half_width], rows[:, half_width:]]


def pack_into(out_ref, tick, per_expert, slices, tables, pairs):
    devices, block, half_width = out_ref.shape
    rows = devices * block
    total = jnp.zeros((rows, half_width), jnp.float32)
    for direction, halves in enumerate(pairs):
        place, _ = placing(
            tables[2 * direction], tables[2 * direction + 1], tick, direction, rows, per_expert, slices
        )
        side = half_of(rows, place.shape[1], per_expert)
        for half in range(2):
            total = total + exact_dot(jnp.where(side == half, place, 0.0), halves[half])
    out_ref[...] = total.astype(jnp.bfloat16).reshape(out_ref.shape)


def first_pack_kernel(tick, per_expert, slices, *refs):
    operands, out_ref, local, sem = refs[:6], refs[6], refs[7:13], refs[13]
    copies = [
        pltpu.make_async_copy(source, target, sem.at[index])
        for index, (source, target) in enumerate(zip(operands, local))
    ]
    for copy in copies:
        copy.start()
    for copy in copies:
        copy.wait()
    pairs = [split_rows(tokens_ref[0]) for tokens_ref in local[4:]]
    pack_into(out_ref, tick, per_expert, slices, local[:4], pairs)


def first_pack(tick, devices, per_expert, slices, routing, fwd, bwd, beside):
    operands = [*routing, fwd, bwd]
    return pl.pallas_call(
        functools.partial(first_pack_kernel, tick, per_expert, slices),
        out_shape=pltpu.VMEM((devices, 4 * per_expert, fwd.shape[-1] // 2), jnp.bfloat16),
        in_specs=[HBM] * len(operands),
        out_specs=VMEM,
        scratch_shapes=[pltpu.VMEM(operand.shape, operand.dtype) for operand in operands]
        + [pltpu.SemaphoreType.DMA((len(operands),))],
        compiler_params=pltpu.CompilerParams(vmem_limit_bytes=SMALL_VMEM),
        cost_estimate=pl.CostEstimate(flops=beside, bytes_accessed=0, transcendentals=0),
    )(*(pltpu.with_memory_space_constraint(operand, pltpu.HBM) for operand in operands))


def later_pack_kernel(tick, per_expert, slices, *refs):
    tables, section_ref, enter_refs, out_ref = refs[:4], refs[4], refs[5:7], refs[7]
    pack_into(out_ref, tick, per_expert, slices, tables, arriving(section_ref, enter_refs))


def later_pack(tick, devices, per_expert, slices, routing, arrived, *entering):
    return pl.pallas_call(
        functools.partial(later_pack_kernel, tick, per_expert, slices),
        out_shape=pltpu.VMEM((devices, 4 * per_expert, arrived.shape[-1]), jnp.bfloat16),
        in_specs=[VMEM] * 7,
        out_specs=VMEM,
        compiler_params=pltpu.CompilerParams(vmem_limit_bytes=SMALL_VMEM),
    )(*routing, arrived, *entering)


def mixed_halves(tick, per_expert, slices, tables, back_ref, pairs):
    devices, block, half_width = back_ref.shape
    rows = devices * block
    back = back_ref[...].reshape(rows, half_width)
    results = []
    for direction, halves in enumerate(pairs):
        _, weight = placing(
            tables[2 * direction], tables[2 * direction + 1], tick, direction, rows, per_expert, slices
        )
        side = half_of(rows, weight.shape[1], per_expert)
        sides = jnp.concatenate(
            [jnp.where(side == half, weight, 0.0) for half in range(2)], axis=1
        )
        high = sides.astype(jnp.bfloat16)
        left = sides - high.astype(jnp.float32)
        middle = left.astype(jnp.bfloat16)
        low = (left - middle.astype(jnp.float32)).astype(jnp.bfloat16)
        mixed = jnp.concatenate(halves, axis=0).astype(jnp.float32)
        for term in (low, middle, high):
            mixed = mixed + lax.dot_general(
                term, back, (((0,), (0,)), ((), ())), preferred_element_type=jnp.float32
            )
        results.append(mixed.astype(jnp.bfloat16))
    return results


def relay_kernel(tick, per_expert, slices, *refs):
    tables, back_ref, token_refs, section_ref, next_refs = refs[:4], refs[4], refs[5:7], refs[7], refs[8:]
    half_width = back_ref.shape[2]
    section, last = lax.axis_index("section"), lax.axis_size("section") - 1
    pairs = [split_rows(tokens_ref[0]) for tokens_ref in token_refs]
    results = mixed_halves(tick, per_expert, slices, tables, back_ref, pairs)
    section_ref[...] = jnp.zeros_like(section_ref)
    for result, next_ref in zip(results, next_refs):
        count = result.shape[0] // 2
        for half in range(2):
            next_ref[:, half * half_width : (half + 1) * half_width] = result[
                half * count : (half + 1) * count
            ]

    @pl.when(section < last)
    def _():
        section_ref[jnp.minimum(section + 1, last)] = results[0]

    @pl.when(section > 0)
    def _():
        section_ref[jnp.maximum(section - 1, 0)] = results[1]


def relay(tick, per_expert, slices, routing, back, fwd, bwd):
    tokens, width = fwd.shape[-2:]
    sections = lax.axis_size("section")
    return pl.pallas_call(
        functools.partial(relay_kernel, tick, per_expert, slices),
        out_shape=[pltpu.VMEM((sections, 2 * tokens, width // 2), jnp.bfloat16)]
        + [pltpu.VMEM((tokens, width), jnp.bfloat16)] * 2,
        in_specs=[VMEM] * 7,
        out_specs=[VMEM] * 3,
        compiler_params=pltpu.CompilerParams(vmem_limit_bytes=SMALL_VMEM),
    )(*routing, back, fwd, bwd)


def finish_kernel(tick, per_expert, slices, *refs):
    tables, back_ref, section_ref, enter_refs, earlier_refs, out_refs = (
        refs[:4], refs[4], refs[5], refs[6:8], refs[8:10], refs[10:],
    )
    half_width = back_ref.shape[2]
    pairs = arriving(section_ref, enter_refs)
    results = mixed_halves(tick, per_expert, slices, tables, back_ref, pairs)
    for result, earlier_ref, out_ref in zip(results, earlier_refs, out_refs):
        count = result.shape[0] // 2
        out_ref[0, 0] = earlier_ref[...]
        for half in range(2):
            out_ref[tick, 0, :, half * half_width : (half + 1) * half_width] = result[
                half * count : (half + 1) * count
            ]


def finish(tick, per_expert, slices, routing, back, arrived, *others):
    tokens, width = others[0].shape
    return pl.pallas_call(
        functools.partial(finish_kernel, tick, per_expert, slices),
        out_shape=[jax.ShapeDtypeStruct((TICKS, 1, tokens, width), jnp.bfloat16)] * 2,
        in_specs=[VMEM] * 10,
        out_specs=[VMEM] * 2,
        compiler_params=pltpu.CompilerParams(vmem_limit_bytes=SMALL_VMEM),
    )(*routing, back, arrived, *others)


def expert_kernel(tick, rows_ref, saved_ref, w_in, w_out, out_ref, *rest):
    saved, slot_rows, joined, parts, saved_sem = rest[-5:]
    devices, block, half_width = rows_ref.shape
    per_expert = block // 4
    slots = devices * per_expert
    width, both = w_in.shape
    hidden_units = both // 2
    rows = devices * block

    saved_copy = pltpu.make_async_copy(saved_ref.at[tick, 0, 0], saved, saved_sem)
    saved_copy.start()

    received = rows_ref[...].reshape(rows, half_width)
    slot = lax.broadcasted_iota(jnp.int32, (2 * slots, rows), 0)
    row = lax.broadcasted_iota(jnp.int32, (2 * slots, rows), 1)
    home = (slot % slots) // per_expert * block + slot // slots * per_expert + slot % per_expert
    for half in range(2):
        pick = jnp.where(row == home + half * 2 * per_expert, 1.0, 0.0)
        slot_rows[:, half * half_width : (half + 1) * half_width] = exact_dot(
            pick, received
        ).astype(jnp.bfloat16)

    grad = lax.dot_general(
        slot_rows[slots:],
        w_out[...],
        (((1,), (1,)), ((), ())),
        preferred_element_type=jnp.float32,
    )
    gate_up = jnp.dot(slot_rows[:slots], w_in[...], preferred_element_type=jnp.float32)
    saved_copy.wait()
    gate_pre = saved[:, :hidden_units]
    sigma = jax.nn.sigmoid(gate_pre)
    slope = sigma * (1.0 + gate_pre * (1.0 - sigma))
    joined[:, :hidden_units] = (grad * saved[:, hidden_units:] * slope).astype(jnp.bfloat16)
    joined[:, hidden_units:] = (grad * (gate_pre * sigma)).astype(jnp.bfloat16)
    gate = gate_up[:, :hidden_units]
    hidden = (gate * jax.nn.sigmoid(gate) * gate_up[:, hidden_units:]).astype(jnp.bfloat16)
    parts[slots:] = lax.dot_general(
        joined[...], w_in[...], (((1,), (1,)), ((), ())), preferred_element_type=jnp.float32
    ).astype(jnp.bfloat16)
    parts[:slots] = jnp.dot(hidden, w_out[...], preferred_element_type=jnp.float32).astype(
        jnp.bfloat16
    )

    row = lax.broadcasted_iota(jnp.int32, (rows, 2 * slots), 0)
    slot = lax.broadcasted_iota(jnp.int32, (rows, 2 * slots), 1)
    home = (slot % slots) // per_expert * block + slot // slots * per_expert + slot % per_expert
    total = jnp.zeros((rows, half_width), jnp.float32)
    for half in range(2):
        spread = jnp.where(row == home + half * 2 * per_expert, 1.0, 0.0)
        total = total + exact_dot(spread, parts[:, half * half_width : (half + 1) * half_width])
    out_ref[...] = total.astype(jnp.bfloat16).reshape(out_ref.shape)


def expert_step(tick, rows, saved_pre, w_in, w_out):
    width, both = w_in.shape
    slots = saved_pre.shape[3]
    return pl.pallas_call(
        functools.partial(expert_kernel, tick),
        out_shape=pltpu.VMEM(rows.shape, jnp.bfloat16),
        in_specs=[VMEM, HBM, VMEM, VMEM],
        out_specs=VMEM,
        scratch_shapes=[
            pltpu.VMEM((slots, both), jnp.float32),
            pltpu.VMEM((2 * slots, width), jnp.bfloat16),
            pltpu.VMEM((slots, both), jnp.bfloat16),
            pltpu.VMEM((2 * slots, width), jnp.bfloat16),
            pltpu.SemaphoreType.DMA,
        ],
        compiler_params=pltpu.CompilerParams(vmem_limit_bytes=EXPERT_VMEM),
        cost_estimate=pl.CostEstimate(
            flops=12 * slots * width * (both // 2),
            bytes_accessed=0,
            transcendentals=0,
        ),
    )(rows, pltpu.with_memory_space_constraint(saved_pre, pltpu.HBM), w_in, w_out)


def exchange(array, axis):
    return lax.all_to_all(array, axis, split_axis=0, concat_axis=0, tiled=True)


def shards(
    fwd_act,
    fwd_enter,
    bwd_grad,
    bwd_enter,
    w_in,
    w_out,
    fwd_route,
    fwd_gate,
    bwd_route,
    bwd_gate,
    saved_pre,
):
    devices = lax.axis_size("expert")
    slices = FF // w_out.shape[2]
    per_expert = saved_pre.shape[3] // devices
    routing = [
        jnp.swapaxes(table, 2, 3) for table in (fwd_route, fwd_gate, bwd_route, bwd_gate)
    ]
    beside = BESIDE * (w_in.size + w_out.size)
    w_in, w_out = (
        pltpu.with_memory_space_constraint(w.reshape(w.shape[2:]), pltpu.VMEM) for w in (w_in, w_out)
    )
    sent = first_pack(0, devices, per_expert, slices, routing, fwd_act, bwd_grad, beside)
    parts = expert_step(0, exchange(sent, "expert"), saved_pre, w_in, w_out)
    moved, fwd_next, bwd_next = relay(
        0, per_expert, slices, routing, exchange(parts, "expert"), fwd_act, bwd_grad
    )
    arrived = exchange(moved, "section")
    sent = later_pack(1, devices, per_expert, slices, routing, arrived, fwd_enter, bwd_enter)
    parts = expert_step(1, exchange(sent, "expert"), saved_pre, w_in, w_out)
    return finish(
        1, per_expert, slices, routing, exchange(parts, "expert"), arrived,
        fwd_enter, bwd_enter, fwd_next, bwd_next,
    )


def solution(mesh):
    placed = (
        P("section", "expert", None),
        P("expert", None),
        P("section", "expert", None),
        P("expert", None),
        P("section", "expert", None, None),
        P("section", "expert", None, None),
        P(None, "section", "expert", None),
        P(None, "section", "expert", None),
        P(None, "section", "expert", None),
        P(None, "section", "expert", None),
        P(None, "section", "expert", None, None),
    )
    return jax.shard_map(
        shards,
        mesh=mesh,
        in_specs=placed,
        out_specs=(P(None, "section", "expert", None), P(None, "section", "expert", None)),
        check_vma=False,
    )
```

```python
import functools

import jax
import jax.numpy as jnp
from jax import lax
from jax.experimental import pallas as pl
from jax.experimental.pallas import tpu as pltpu
from jax.sharding import PartitionSpec as P

FF = 1024
TICKS = 2
EXPERT_VMEM = 16 * 1024 * 1024
BESIDE = 2000
COLUMNS = 256
SMALL_VMEM = 8 * 1024 * 1024
VMEM = pl.BlockSpec(memory_space=pltpu.VMEM)
HBM = pl.BlockSpec(memory_space=pltpu.HBM)


def exact_dot(one_hot, values):
    return jnp.dot(one_hot.astype(jnp.bfloat16), values, preferred_element_type=jnp.float32)


def placing(route_ref, gate_ref, tick, direction, rows, per_expert, slices):
    route = route_ref[tick, 0]
    gate = gate_ref[tick, 0]
    top, tokens = route.shape
    block = 4 * per_expert
    row = lax.broadcasted_iota(jnp.int32, (rows, tokens), 0)
    expert = row // (block * slices)
    mine = (row // per_expert) % 2 == direction
    hit = jnp.zeros((rows, tokens), jnp.float32)
    weight = jnp.zeros((rows, tokens), jnp.float32)
    for column in range(top):
        named = route[column : column + 1, :] == expert
        hit = jnp.where(named, 1.0, hit)
        weight = jnp.where(named, gate[column : column + 1, :], weight)
    lane = lax.broadcasted_iota(jnp.int32, (rows, tokens), 1)
    rank = jnp.zeros((rows, tokens), jnp.float32)
    for token in range(tokens - 1):
        rank = rank + jnp.where(lane > token, hit[:, token : token + 1], 0.0)
    place = jnp.where(
        mine & (hit > 0.0) & (rank.astype(jnp.int32) == row % per_expert), 1.0, 0.0
    )
    return place, weight * place


def half_of(rows, width, per_expert):
    row = lax.broadcasted_iota(jnp.int32, (rows, width), 0)
    return (row // (2 * per_expert)) % 2


def whole_rows(rows_ref, index):
    block = rows_ref[index]
    count = block.shape[0] // 2
    return block[:count], block[count:]


def arriving(section_ref, enter_refs):
    section, last = lax.axis_index("section"), lax.axis_size("section") - 1
    pairs = []
    for source, edge, enter_ref in (
        (section - 1, section == 0, enter_refs[0]),
        (section + 1, section == last, enter_refs[1]),
    ):
        halves = whole_rows(section_ref, jnp.clip(source, 0, last))
        half_width = halves[0].shape[1]
        pairs.append(
            [
                jnp.where(edge, enter_ref[:, half * half_width : (half + 1) * half_width], halves[half])
                for half in range(2)
            ]
        )
    return pairs


def split_rows(rows):
    half_width = rows.shape[-1] // 2
    return [rows[:, :half_width], rows[:, half_width:]]


def pack_into(out_ref, tick, per_expert, slices, tables, pairs):
    devices, block, half_width = out_ref.shape
    rows = devices * block
    total = jnp.zeros((rows, half_width), jnp.float32)
    for direction, halves in enumerate(pairs):
        place, _ = placing(
            tables[2 * direction], tables[2 * direction + 1], tick, direction, rows, per_expert, slices
        )
        side = half_of(rows, place.shape[1], per_expert)
        for half in range(2):
            total = total + exact_dot(jnp.where(side == half, place, 0.0), halves[half])
    out_ref[...] = total.astype(jnp.bfloat16).reshape(out_ref.shape)


def first_pack_kernel(tick, per_expert, slices, *refs):
    operands, out_ref, local, sem = refs[:6], refs[6], refs[7:13], refs[13]
    copies = [
        pltpu.make_async_copy(source, target, sem.at[index])
        for index, (source, target) in enumerate(zip(operands, local))
    ]
    for copy in copies:
        copy.start()
    for copy in copies:
        copy.wait()
    pairs = [split_rows(tokens_ref[0]) for tokens_ref in local[4:]]
    pack_into(out_ref, tick, per_expert, slices, local[:4], pairs)


def first_pack(tick, devices, per_expert, slices, routing, fwd, bwd, beside):
    operands = [*routing, fwd, bwd]
    return pl.pallas_call(
        functools.partial(first_pack_kernel, tick, per_expert, slices),
        out_shape=pltpu.VMEM((devices, 4 * per_expert, fwd.shape[-1] // 2), jnp.bfloat16),
        in_specs=[HBM] * len(operands),
        out_specs=VMEM,
        scratch_shapes=[pltpu.VMEM(operand.shape, operand.dtype) for operand in operands]
        + [pltpu.SemaphoreType.DMA((len(operands),))],
        compiler_params=pltpu.CompilerParams(vmem_limit_bytes=SMALL_VMEM),
        cost_estimate=pl.CostEstimate(flops=beside, bytes_accessed=0, transcendentals=0),
    )(*(pltpu.with_memory_space_constraint(operand, pltpu.HBM) for operand in operands))


def later_pack_kernel(tick, per_expert, slices, *refs):
    tables, section_ref, enter_refs, out_ref = refs[:4], refs[4], refs[5:7], refs[7]
    pack_into(out_ref, tick, per_expert, slices, tables, arriving(section_ref, enter_refs))


def later_pack(tick, devices, per_expert, slices, routing, arrived, *entering):
    return pl.pallas_call(
        functools.partial(later_pack_kernel, tick, per_expert, slices),
        out_shape=pltpu.VMEM((devices, 4 * per_expert, arrived.shape[-1]), jnp.bfloat16),
        in_specs=[VMEM] * 7,
        out_specs=VMEM,
        compiler_params=pltpu.CompilerParams(vmem_limit_bytes=SMALL_VMEM),
    )(*routing, arrived, *entering)


def mixed_halves(tick, per_expert, slices, tables, back_ref, pairs):
    devices, block, half_width = back_ref.shape
    rows = devices * block
    back = back_ref[...].reshape(rows, half_width)
    results = []
    for direction, halves in enumerate(pairs):
        _, weight = placing(
            tables[2 * direction], tables[2 * direction + 1], tick, direction, rows, per_expert, slices
        )
        side = half_of(rows, weight.shape[1], per_expert)
        sides = jnp.concatenate(
            [jnp.where(side == half, weight, 0.0) for half in range(2)], axis=1
        )
        high = sides.astype(jnp.bfloat16)
        left = sides - high.astype(jnp.float32)
        middle = left.astype(jnp.bfloat16)
        low = (left - middle.astype(jnp.float32)).astype(jnp.bfloat16)
        mixed = jnp.concatenate(halves, axis=0).astype(jnp.float32)
        for term in (low, middle, high):
            mixed = mixed + lax.dot_general(
                term, back, (((0,), (0,)), ((), ())), preferred_element_type=jnp.float32
            )
        results.append(mixed.astype(jnp.bfloat16))
    return results


def relay_kernel(tick, per_expert, slices, *refs):
    tables, back_ref, token_refs, section_ref, next_refs = refs[:4], refs[4], refs[5:7], refs[7], refs[8:]
    half_width = back_ref.shape[2]
    section, last = lax.axis_index("section"), lax.axis_size("section") - 1
    pairs = [split_rows(tokens_ref[0]) for tokens_ref in token_refs]
    results = mixed_halves(tick, per_expert, slices, tables, back_ref, pairs)
    section_ref[...] = jnp.zeros_like(section_ref)
    for result, next_ref in zip(results, next_refs):
        count = result.shape[0] // 2
        for half in range(2):
            next_ref[:, half * half_width : (half + 1) * half_width] = result[
                half * count : (half + 1) * count
            ]

    @pl.when(section < last)
    def _():
        section_ref[jnp.minimum(section + 1, last)] = results[0]

    @pl.when(section > 0)
    def _():
        section_ref[jnp.maximum(section - 1, 0)] = results[1]


def relay(tick, per_expert, slices, routing, back, fwd, bwd):
    tokens, width = fwd.shape[-2:]
    sections = lax.axis_size("section")
    return pl.pallas_call(
        functools.partial(relay_kernel, tick, per_expert, slices),
        out_shape=[pltpu.VMEM((sections, 2 * tokens, width // 2), jnp.bfloat16)]
        + [pltpu.VMEM((tokens, width), jnp.bfloat16)] * 2,
        in_specs=[VMEM] * 7,
        out_specs=[VMEM] * 3,
        compiler_params=pltpu.CompilerParams(vmem_limit_bytes=SMALL_VMEM),
    )(*routing, back, fwd, bwd)


def finish_kernel(tick, per_expert, slices, *refs):
    tables, back_ref, section_ref, enter_refs, earlier_refs, out_refs, new_refs, sem = (
        refs[:4], refs[4], refs[5], refs[6:8], refs[8:10], refs[10:12], refs[12:14], refs[14],
    )
    half_width = back_ref.shape[2]
    copies = [
        pltpu.make_async_copy(source, out_ref.at[place, 0], sem.at[place, direction])
        for place, sources in ((0, earlier_refs), (tick, new_refs))
        for direction, (source, out_ref) in enumerate(zip(sources, out_refs))
    ]
    for copy in copies[:2]:
        copy.start()
    pairs = arriving(section_ref, enter_refs)
    results = mixed_halves(tick, per_expert, slices, tables, back_ref, pairs)
    for result, new_ref, copy in zip(results, new_refs, copies[2:]):
        count = result.shape[0] // 2
        for half in range(2):
            new_ref[:, half * half_width : (half + 1) * half_width] = result[
                half * count : (half + 1) * count
            ]
        copy.start()
    for copy in copies:
        copy.wait()


def finish(tick, per_expert, slices, routing, back, arrived, *others):
    tokens, width = others[0].shape
    return pl.pallas_call(
        functools.partial(finish_kernel, tick, per_expert, slices),
        out_shape=[jax.ShapeDtypeStruct((TICKS, 1, tokens, width), jnp.bfloat16)] * 2,
        in_specs=[VMEM] * 10,
        out_specs=[HBM] * 2,
        scratch_shapes=[pltpu.VMEM((tokens, width), jnp.bfloat16)] * 2
        + [pltpu.SemaphoreType.DMA((TICKS, 2))],
        compiler_params=pltpu.CompilerParams(vmem_limit_bytes=SMALL_VMEM),
    )(*routing, back, arrived, *others)


def expert_kernel(tick, rows_ref, saved_ref, w_in, w_out, out_ref, *rest):
    saved, slot_rows, joined, hidden, saved_sem = rest
    devices, block, half_width = rows_ref.shape
    per_expert = block // 4
    slots = devices * per_expert
    width, both = w_in.shape
    hidden_units = both // 2
    rows = devices * block

    saved_copy = pltpu.make_async_copy(saved_ref.at[tick, 0, 0], saved, saved_sem)
    saved_copy.start()

    received = rows_ref[...].reshape(rows, half_width)
    slot = lax.broadcasted_iota(jnp.int32, (2 * slots, rows), 0)
    row = lax.broadcasted_iota(jnp.int32, (2 * slots, rows), 1)
    home = (slot % slots) // per_expert * block + slot // slots * per_expert + slot % per_expert
    for half in range(2):
        pick = jnp.where(row == home + half * 2 * per_expert, 1.0, 0.0)
        slot_rows[:, half * half_width : (half + 1) * half_width] = exact_dot(
            pick, received
        ).astype(jnp.bfloat16)

    saved_copy.wait()
    chunk = min(hidden_units, COLUMNS)
    for start in range(0, hidden_units, chunk):
        at, up_at = (pl.ds(start + side, chunk) for side in (0, hidden_units))
        grad = lax.dot_general(
            slot_rows[slots:],
            w_out[at, :],
            (((1,), (1,)), ((), ())),
            preferred_element_type=jnp.float32,
        )
        gate = jnp.dot(slot_rows[:slots], w_in[:, at], preferred_element_type=jnp.float32)
        up = jnp.dot(slot_rows[:slots], w_in[:, up_at], preferred_element_type=jnp.float32)
        gate_pre = saved[:, at]
        sigma = jax.nn.sigmoid(gate_pre)
        slope = sigma * (1.0 + gate_pre * (1.0 - sigma))
        joined[:, at] = (grad * saved[:, up_at] * slope).astype(jnp.bfloat16)
        joined[:, up_at] = (grad * (gate_pre * sigma)).astype(jnp.bfloat16)
        hidden[:, at] = (gate * jax.nn.sigmoid(gate) * up).astype(jnp.bfloat16)

    row = lax.broadcasted_iota(jnp.int32, (rows, 4 * slots), 0)
    line = lax.broadcasted_iota(jnp.int32, (rows, 4 * slots), 1)
    slot = line % (2 * slots)
    home = (slot % slots) // per_expert * block + slot // slots * per_expert + slot % per_expert
    spread = jnp.where(row == home + line // (2 * slots) * 2 * per_expert, 1.0, 0.0)
    for start in range(0, half_width, COLUMNS):
        parts = []
        for half in range(2):
            at = pl.ds(half * half_width + start, min(COLUMNS, half_width - start))
            back = lax.dot_general(
                joined[...], w_in[at, :], (((1,), (1,)), ((), ())), preferred_element_type=jnp.float32
            )
            ahead = jnp.dot(hidden[...], w_out[:, at], preferred_element_type=jnp.float32)
            parts += [ahead.astype(jnp.bfloat16), back.astype(jnp.bfloat16)]
        laid = exact_dot(spread, jnp.concatenate(parts, axis=0))
        out_ref[:, :, start : start + laid.shape[1]] = laid.astype(jnp.bfloat16).reshape(
            devices, block, laid.shape[1]
        )


def expert_step(tick, rows, saved_pre, w_in, w_out):
    width, both = w_in.shape
    slots = saved_pre.shape[3]
    return pl.pallas_call(
        functools.partial(expert_kernel, tick),
        out_shape=pltpu.VMEM(rows.shape, jnp.bfloat16),
        in_specs=[VMEM, HBM, VMEM, VMEM],
        out_specs=VMEM,
        scratch_shapes=[
            pltpu.VMEM((slots, both), jnp.float32),
            pltpu.VMEM((2 * slots, width), jnp.bfloat16),
            pltpu.VMEM((slots, both), jnp.bfloat16),
            pltpu.VMEM((slots, both // 2), jnp.bfloat16),
            pltpu.SemaphoreType.DMA,
        ],
        compiler_params=pltpu.CompilerParams(vmem_limit_bytes=EXPERT_VMEM),
        cost_estimate=pl.CostEstimate(
            flops=12 * slots * width * (both // 2),
            bytes_accessed=0,
            transcendentals=0,
        ),
    )(rows, pltpu.with_memory_space_constraint(saved_pre, pltpu.HBM), w_in, w_out)


def exchange(array, axis):
    return lax.all_to_all(array, axis, split_axis=0, concat_axis=0, tiled=True)


def shards(
    fwd_act,
    fwd_enter,
    bwd_grad,
    bwd_enter,
    w_in,
    w_out,
    fwd_route,
    fwd_gate,
    bwd_route,
    bwd_gate,
    saved_pre,
):
    devices = lax.axis_size("expert")
    slices = FF // w_out.shape[2]
    per_expert = saved_pre.shape[3] // devices
    routing = [
        jnp.swapaxes(table, 2, 3) for table in (fwd_route, fwd_gate, bwd_route, bwd_gate)
    ]
    beside = BESIDE * (w_in.size + w_out.size)
    w_in, w_out = (
        pltpu.with_memory_space_constraint(w.reshape(w.shape[2:]), pltpu.VMEM) for w in (w_in, w_out)
    )
    sent = first_pack(0, devices, per_expert, slices, routing, fwd_act, bwd_grad, beside)
    parts = expert_step(0, exchange(sent, "expert"), saved_pre, w_in, w_out)
    moved, fwd_next, bwd_next = relay(
        0, per_expert, slices, routing, exchange(parts, "expert"), fwd_act, bwd_grad
    )
    arrived = exchange(moved, "section")
    sent = later_pack(1, devices, per_expert, slices, routing, arrived, fwd_enter, bwd_enter)
    parts = expert_step(1, exchange(sent, "expert"), saved_pre, w_in, w_out)
    return finish(
        1, per_expert, slices, routing, exchange(parts, "expert"), arrived,
        fwd_enter, bwd_enter, fwd_next, bwd_next,
    )


def solution(mesh):
    placed = (
        P("section", "expert", None),
        P("expert", None),
        P("section", "expert", None),
        P("expert", None),
        P("section", "expert", None, None),
        P("section", "expert", None, None),
        P(None, "section", "expert", None),
        P(None, "section", "expert", None),
        P(None, "section", "expert", None),
        P(None, "section", "expert", None),
        P(None, "section", "expert", None, None),
    )
    return jax.shard_map(
        shards,
        mesh=mesh,
        in_specs=placed,
        out_specs=(P(None, "section", "expert", None), P(None, "section", "expert", None)),
        check_vma=False,
    )
```

```python
import functools

import jax
import jax.numpy as jnp
from jax import lax
from jax.experimental import pallas as pl
from jax.experimental.pallas import tpu as pltpu
from jax.sharding import PartitionSpec as P

FF = 1024
TICKS = 2
EXPERT_VMEM = 16 * 1024 * 1024
BESIDE = 2000
SMALL_VMEM = 8 * 1024 * 1024
VMEM = pl.BlockSpec(memory_space=pltpu.VMEM)
HBM = pl.BlockSpec(memory_space=pltpu.HBM)


def exact_dot(one_hot, values):
    return jnp.dot(one_hot.astype(jnp.bfloat16), values, preferred_element_type=jnp.float32)


def placing(route_ref, gate_ref, tick, direction, rows, per_expert, slices):
    route = route_ref[tick, 0]
    gate = gate_ref[tick, 0]
    top, tokens = route.shape
    block = 4 * per_expert
    row = lax.broadcasted_iota(jnp.int32, (rows, tokens), 0)
    expert = row // (block * slices)
    mine = (row // per_expert) % 2 == direction
    hit = jnp.zeros((rows, tokens), jnp.float32)
    weight = jnp.zeros((rows, tokens), jnp.float32)
    for column in range(top):
        named = route[column : column + 1, :] == expert
        hit = jnp.where(named, 1.0, hit)
        weight = jnp.where(named, gate[column : column + 1, :], weight)
    lane = lax.broadcasted_iota(jnp.int32, (rows, tokens), 1)
    rank = jnp.zeros((rows, tokens), jnp.float32)
    for token in range(tokens - 1):
        rank = rank + jnp.where(lane > token, hit[:, token : token + 1], 0.0)
    place = jnp.where(
        mine & (hit > 0.0) & (rank.astype(jnp.int32) == row % per_expert), 1.0, 0.0
    )
    return place, weight * place


def half_of(rows, width, per_expert):
    row = lax.broadcasted_iota(jnp.int32, (rows, width), 0)
    return (row // (2 * per_expert)) % 2


def whole_rows(rows_ref, index):
    block = rows_ref[index]
    count = block.shape[0] // 2
    return block[:count], block[count:]


def arriving(section_ref, enter_refs):
    section, last = lax.axis_index("section"), lax.axis_size("section") - 1
    pairs = []
    for source, edge, enter_ref in (
        (section - 1, section == 0, enter_refs[0]),
        (section + 1, section == last, enter_refs[1]),
    ):
        halves = whole_rows(section_ref, jnp.clip(source, 0, last))
        half_width = halves[0].shape[1]
        pairs.append(
            [
                jnp.where(edge, enter_ref[:, half * half_width : (half + 1) * half_width], halves[half])
                for half in range(2)
            ]
        )
    return pairs


def split_rows(rows):
    half_width = rows.shape[-1] // 2
    return [rows[:, :half_width], rows[:, half_width:]]


def pack_into(out_ref, tick, per_expert, slices, tables, pairs):
    devices, block, half_width = out_ref.shape
    rows = devices * block
    places, values = [], []
    for direction, halves in enumerate(pairs):
        place, _ = placing(
            tables[2 * direction], tables[2 * direction + 1], tick, direction, rows, per_expert, slices
        )
        side = half_of(rows, place.shape[1], per_expert)
        places += [jnp.where(side == half, place, 0.0) for half in range(2)]
        values += [value.astype(jnp.float32) for value in halves]
    total = exact_dot(
        jnp.concatenate(places, axis=1), jnp.concatenate(values, axis=0).astype(jnp.bfloat16)
    )
    out_ref[...] = total.astype(jnp.bfloat16).reshape(out_ref.shape)


def first_pack_kernel(tick, per_expert, slices, *refs):
    operands, out_ref, local, sem = refs[:6], refs[6], refs[7:13], refs[13]
    copies = [
        pltpu.make_async_copy(source, target, sem.at[index])
        for index, (source, target) in enumerate(zip(operands, local))
    ]
    for copy in copies:
        copy.start()
    for copy in copies:
        copy.wait()
    pairs = [split_rows(tokens_ref[0]) for tokens_ref in local[4:]]
    pack_into(out_ref, tick, per_expert, slices, local[:4], pairs)


def first_pack(tick, devices, per_expert, slices, routing, fwd, bwd, beside):
    operands = [*routing, fwd, bwd]
    return pl.pallas_call(
        functools.partial(first_pack_kernel, tick, per_expert, slices),
        out_shape=pltpu.VMEM((devices, 4 * per_expert, fwd.shape[-1] // 2), jnp.bfloat16),
        in_specs=[HBM] * len(operands),
        out_specs=VMEM,
        scratch_shapes=[pltpu.VMEM(operand.shape, operand.dtype) for operand in operands]
        + [pltpu.SemaphoreType.DMA((len(operands),))],
        compiler_params=pltpu.CompilerParams(vmem_limit_bytes=SMALL_VMEM),
        cost_estimate=pl.CostEstimate(flops=beside, bytes_accessed=0, transcendentals=0),
    )(*(pltpu.with_memory_space_constraint(operand, pltpu.HBM) for operand in operands))


def later_pack_kernel(tick, per_expert, slices, *refs):
    tables, section_ref, enter_refs, out_ref = refs[:4], refs[4], refs[5:7], refs[7]
    pack_into(out_ref, tick, per_expert, slices, tables, arriving(section_ref, enter_refs))


def later_pack(tick, devices, per_expert, slices, routing, arrived, *entering):
    return pl.pallas_call(
        functools.partial(later_pack_kernel, tick, per_expert, slices),
        out_shape=pltpu.VMEM((devices, 4 * per_expert, arrived.shape[-1]), jnp.bfloat16),
        in_specs=[VMEM] * 7,
        out_specs=VMEM,
        compiler_params=pltpu.CompilerParams(vmem_limit_bytes=SMALL_VMEM),
    )(*routing, arrived, *entering)


def mixed_halves(tick, per_expert, slices, tables, back_ref, pairs):
    devices, block, half_width = back_ref.shape
    rows = devices * block
    back = back_ref[...].reshape(rows, half_width)
    terms = []
    for direction in range(2):
        _, weight = placing(
            tables[2 * direction], tables[2 * direction + 1], tick, direction, rows, per_expert, slices
        )
        side = half_of(rows, weight.shape[1], per_expert)
        sides = jnp.concatenate(
            [jnp.where(side == half, weight, 0.0) for half in range(2)], axis=1
        )
        high = sides.astype(jnp.bfloat16).astype(jnp.float32)
        middle = (sides - high).astype(jnp.bfloat16).astype(jnp.float32)
        terms += [sides - high - middle, middle, high]
    mixed = lax.dot_general(
        jnp.concatenate(terms, axis=1).astype(jnp.bfloat16),
        back,
        (((0,), (0,)), ((), ())),
        preferred_element_type=jnp.float32,
    )
    results = []
    for direction, halves in enumerate(pairs):
        total = jnp.concatenate([half.astype(jnp.float32) for half in halves], axis=0)
        count = total.shape[0]
        for term in range(3):
            start = (3 * direction + term) * count
            total = total + mixed[start : start + count]
        results.append(total.astype(jnp.bfloat16))
    return results


def relay_kernel(tick, per_expert, slices, *refs):
    tables, back_ref, token_refs, section_ref, next_refs = refs[:4], refs[4], refs[5:7], refs[7], refs[8:]
    half_width = back_ref.shape[2]
    section, last = lax.axis_index("section"), lax.axis_size("section") - 1
    pairs = [split_rows(tokens_ref[0]) for tokens_ref in token_refs]
    results = mixed_halves(tick, per_expert, slices, tables, back_ref, pairs)
    section_ref[...] = jnp.zeros_like(section_ref)
    for result, next_ref in zip(results, next_refs):
        count = result.shape[0] // 2
        for half in range(2):
            next_ref[:, half * half_width : (half + 1) * half_width] = result[
                half * count : (half + 1) * count
            ]

    @pl.when(section < last)
    def _():
        section_ref[jnp.minimum(section + 1, last)] = results[0]

    @pl.when(section > 0)
    def _():
        section_ref[jnp.maximum(section - 1, 0)] = results[1]


def relay(tick, per_expert, slices, routing, back, fwd, bwd):
    tokens, width = fwd.shape[-2:]
    sections = lax.axis_size("section")
    return pl.pallas_call(
        functools.partial(relay_kernel, tick, per_expert, slices),
        out_shape=[pltpu.VMEM((sections, 2 * tokens, width // 2), jnp.bfloat16)]
        + [pltpu.VMEM((tokens, width), jnp.bfloat16)] * 2,
        in_specs=[VMEM] * 7,
        out_specs=[VMEM] * 3,
        compiler_params=pltpu.CompilerParams(vmem_limit_bytes=SMALL_VMEM),
    )(*routing, back, fwd, bwd)


def finish_kernel(tick, per_expert, slices, *refs):
    tables, back_ref, section_ref, enter_refs, earlier_refs, out_refs = (
        refs[:4], refs[4], refs[5], refs[6:8], refs[8:10], refs[10:],
    )
    half_width = back_ref.shape[2]
    pairs = arriving(section_ref, enter_refs)
    results = mixed_halves(tick, per_expert, slices, tables, back_ref, pairs)
    for result, earlier_ref, out_ref in zip(results, earlier_refs, out_refs):
        count = result.shape[0] // 2
        out_ref[0, 0] = earlier_ref[...]
        for half in range(2):
            out_ref[tick, 0, :, half * half_width : (half + 1) * half_width] = result[
                half * count : (half + 1) * count
            ]


def finish(tick, per_expert, slices, routing, back, arrived, *others):
    tokens, width = others[0].shape
    return pl.pallas_call(
        functools.partial(finish_kernel, tick, per_expert, slices),
        out_shape=[jax.ShapeDtypeStruct((TICKS, 1, tokens, width), jnp.bfloat16)] * 2,
        in_specs=[VMEM] * 10,
        out_specs=[VMEM] * 2,
        compiler_params=pltpu.CompilerParams(vmem_limit_bytes=SMALL_VMEM),
    )(*routing, back, arrived, *others)


def home_of(line, slots, per_expert):
    half, direction, slot = line // (2 * slots), line // slots % 2, line % slots
    return (
        slot // per_expert * (4 * per_expert)
        + (2 * half + direction) * per_expert
        + slot % per_expert
    )


def expert_kernel(tick, rows_ref, saved_ref, w_in, w_out, out_ref, *rest):
    saved, slot_rows, joined, parts, saved_sem = rest[-5:]
    devices, block, half_width = rows_ref.shape
    per_expert = block // 4
    slots = devices * per_expert
    width, both = w_in.shape
    hidden_units = both // 2
    rows = devices * block

    saved_copy = pltpu.make_async_copy(saved_ref.at[tick, 0, 0], saved, saved_sem)
    saved_copy.start()

    received = rows_ref[...].reshape(rows, half_width)
    line = lax.broadcasted_iota(jnp.int32, (4 * slots, rows), 0)
    row = lax.broadcasted_iota(jnp.int32, (4 * slots, rows), 1)
    pick = jnp.where(row == home_of(line, slots, per_expert), 1.0, 0.0)
    picked = exact_dot(pick, received).astype(jnp.bfloat16)
    for half in range(2):
        slot_rows[:, half * half_width : (half + 1) * half_width] = picked[
            half * 2 * slots : (half + 1) * 2 * slots
        ]

    grad = lax.dot_general(
        slot_rows[slots:],
        w_out[...],
        (((1,), (1,)), ((), ())),
        preferred_element_type=jnp.float32,
    )
    gate_up = jnp.dot(slot_rows[:slots], w_in[...], preferred_element_type=jnp.float32)
    saved_copy.wait()
    gate_pre = saved[:, :hidden_units]
    sigma = jax.nn.sigmoid(gate_pre)
    slope = sigma * (1.0 + gate_pre * (1.0 - sigma))
    joined[:, :hidden_units] = (grad * saved[:, hidden_units:] * slope).astype(jnp.bfloat16)
    joined[:, hidden_units:] = (grad * (gate_pre * sigma)).astype(jnp.bfloat16)
    gate = gate_up[:, :hidden_units]
    hidden = (gate * jax.nn.sigmoid(gate) * gate_up[:, hidden_units:]).astype(jnp.bfloat16)
    back = lax.dot_general(
        joined[...], w_in[...], (((1,), (1,)), ((), ())), preferred_element_type=jnp.float32
    ).astype(jnp.bfloat16)
    ahead = jnp.dot(hidden, w_out[...], preferred_element_type=jnp.float32).astype(jnp.bfloat16)
    for half in range(2):
        columns = slice(half * half_width, (half + 1) * half_width)
        start = half * 2 * slots
        parts[start : start + slots] = ahead[:, columns]
        parts[start + slots : start + 2 * slots] = back[:, columns]

    row = lax.broadcasted_iota(jnp.int32, (rows, 4 * slots), 0)
    line = lax.broadcasted_iota(jnp.int32, (rows, 4 * slots), 1)
    spread = jnp.where(row == home_of(line, slots, per_expert), 1.0, 0.0)
    out_ref[...] = exact_dot(spread, parts[...]).astype(jnp.bfloat16).reshape(out_ref.shape)


def expert_step(tick, rows, saved_pre, w_in, w_out):
    width, both = w_in.shape
    slots = saved_pre.shape[3]
    return pl.pallas_call(
        functools.partial(expert_kernel, tick),
        out_shape=pltpu.VMEM(rows.shape, jnp.bfloat16),
        in_specs=[VMEM, HBM, VMEM, VMEM],
        out_specs=VMEM,
        scratch_shapes=[
            pltpu.VMEM((slots, both), jnp.float32),
            pltpu.VMEM((2 * slots, width), jnp.bfloat16),
            pltpu.VMEM((slots, both), jnp.bfloat16),
            pltpu.VMEM((4 * slots, width // 2), jnp.bfloat16),
            pltpu.SemaphoreType.DMA,
        ],
        compiler_params=pltpu.CompilerParams(vmem_limit_bytes=EXPERT_VMEM),
        cost_estimate=pl.CostEstimate(
            flops=12 * slots * width * (both // 2),
            bytes_accessed=0,
            transcendentals=0,
        ),
    )(rows, pltpu.with_memory_space_constraint(saved_pre, pltpu.HBM), w_in, w_out)


def exchange(array, axis):
    return lax.all_to_all(array, axis, split_axis=0, concat_axis=0, tiled=True)


def shards(
    fwd_act,
    fwd_enter,
    bwd_grad,
    bwd_enter,
    w_in,
    w_out,
    fwd_route,
    fwd_gate,
    bwd_route,
    bwd_gate,
    saved_pre,
):
    devices = lax.axis_size("expert")
    slices = FF // w_out.shape[2]
    per_expert = saved_pre.shape[3] // devices
    routing = [
        jnp.swapaxes(table, 2, 3) for table in (fwd_route, fwd_gate, bwd_route, bwd_gate)
    ]
    beside = BESIDE * (w_in.size + w_out.size)
    w_in, w_out = (
        pltpu.with_memory_space_constraint(w.reshape(w.shape[2:]), pltpu.VMEM) for w in (w_in, w_out)
    )
    sent = first_pack(0, devices, per_expert, slices, routing, fwd_act, bwd_grad, beside)
    parts = expert_step(0, exchange(sent, "expert"), saved_pre, w_in, w_out)
    moved, fwd_next, bwd_next = relay(
        0, per_expert, slices, routing, exchange(parts, "expert"), fwd_act, bwd_grad
    )
    arrived = exchange(moved, "section")
    sent = later_pack(1, devices, per_expert, slices, routing, arrived, fwd_enter, bwd_enter)
    parts = expert_step(1, exchange(sent, "expert"), saved_pre, w_in, w_out)
    return finish(
        1, per_expert, slices, routing, exchange(parts, "expert"), arrived,
        fwd_enter, bwd_enter, fwd_next, bwd_next,
    )


def solution(mesh):
    placed = (
        P("section", "expert", None),
        P("expert", None),
        P("section", "expert", None),
        P("expert", None),
        P("section", "expert", None, None),
        P("section", "expert", None, None),
        P(None, "section", "expert", None),
        P(None, "section", "expert", None),
        P(None, "section", "expert", None),
        P(None, "section", "expert", None),
        P(None, "section", "expert", None, None),
    )
    return jax.shard_map(
        shards,
        mesh=mesh,
        in_specs=placed,
        out_specs=(P(None, "section", "expert", None), P(None, "section", "expert", None)),
        check_vma=False,
    )
```

```python
import functools

import jax
import jax.numpy as jnp
from jax import lax
from jax.experimental import pallas as pl
from jax.experimental.pallas import tpu as pltpu
from jax.sharding import PartitionSpec as P

FF = 1024
TICKS = 2
EXPERT_VMEM = 16 * 1024 * 1024
BESIDE = 2000
SMALL_VMEM = 8 * 1024 * 1024
VMEM = pl.BlockSpec(memory_space=pltpu.VMEM)
HBM = pl.BlockSpec(memory_space=pltpu.HBM)


def exact_dot(one_hot, values):
    return jnp.dot(one_hot.astype(jnp.bfloat16), values, preferred_element_type=jnp.float32)


def placing(route_ref, gate_ref, tick, direction, rows, per_expert, slices):
    route = route_ref[tick, 0]
    gate = gate_ref[tick, 0]
    top, tokens = route.shape
    block = 4 * per_expert
    row = lax.broadcasted_iota(jnp.int32, (rows, tokens), 0)
    expert = row // (block * slices)
    mine = (row // per_expert) % 2 == direction
    hit = jnp.zeros((rows, tokens), jnp.float32)
    weight = jnp.zeros((rows, tokens), jnp.float32)
    for column in range(top):
        named = route[column : column + 1, :] == expert
        hit = jnp.where(named, 1.0, hit)
        weight = jnp.where(named, gate[column : column + 1, :], weight)
    lane = lax.broadcasted_iota(jnp.int32, (rows, tokens), 1)
    rank = jnp.zeros((rows, tokens), jnp.float32)
    for token in range(tokens - 1):
        rank = rank + jnp.where(lane > token, hit[:, token : token + 1], 0.0)
    place = jnp.where(
        mine & (hit > 0.0) & (rank.astype(jnp.int32) == row % per_expert), 1.0, 0.0
    )
    return place, weight * place


def half_of(rows, width, per_expert):
    row = lax.broadcasted_iota(jnp.int32, (rows, width), 0)
    return (row // (2 * per_expert)) % 2


def whole_rows(rows_ref, index):
    block = rows_ref[index]
    count = block.shape[0] // 2
    return block[:count], block[count:]


def arriving(section_ref, enter_refs):
    section, last = lax.axis_index("section"), lax.axis_size("section") - 1
    pairs = []
    for source, edge, enter_ref in (
        (section - 1, section == 0, enter_refs[0]),
        (section + 1, section == last, enter_refs[1]),
    ):
        halves = whole_rows(section_ref, jnp.clip(source, 0, last))
        half_width = halves[0].shape[1]
        pairs.append(
            [
                jnp.where(edge, enter_ref[:, half * half_width : (half + 1) * half_width], halves[half])
                for half in range(2)
            ]
        )
    return pairs


def split_rows(rows):
    half_width = rows.shape[-1] // 2
    return [rows[:, :half_width], rows[:, half_width:]]


def pack_into(out_ref, tick, per_expert, slices, tables, pairs):
    devices, block, half_width = out_ref.shape
    rows = devices * block
    places, values = [], []
    for direction, halves in enumerate(pairs):
        place, _ = placing(
            tables[2 * direction], tables[2 * direction + 1], tick, direction, rows, per_expert, slices
        )
        side = half_of(rows, place.shape[1], per_expert)
        places += [jnp.where(side == half, place, 0.0) for half in range(2)]
        values += [value.astype(jnp.float32) for value in halves]
    total = exact_dot(
        jnp.concatenate(places, axis=1), jnp.concatenate(values, axis=0).astype(jnp.bfloat16)
    )
    out_ref[...] = total.astype(jnp.bfloat16).reshape(out_ref.shape)


def first_pack_kernel(tick, per_expert, slices, *refs):
    operands, out_ref, local, sem = refs[:6], refs[6], refs[7:13], refs[13]
    copies = [
        pltpu.make_async_copy(source, target, sem.at[index])
        for index, (source, target) in enumerate(zip(operands, local))
    ]
    for copy in copies:
        copy.start()
    for copy in copies:
        copy.wait()
    pairs = [split_rows(tokens_ref[0]) for tokens_ref in local[4:]]
    pack_into(out_ref, tick, per_expert, slices, local[:4], pairs)


def first_pack(tick, devices, per_expert, slices, routing, fwd, bwd, beside):
    operands = [*routing, fwd, bwd]
    return pl.pallas_call(
        functools.partial(first_pack_kernel, tick, per_expert, slices),
        out_shape=pltpu.VMEM((devices, 4 * per_expert, fwd.shape[-1] // 2), jnp.bfloat16),
        in_specs=[HBM] * len(operands),
        out_specs=VMEM,
        scratch_shapes=[pltpu.VMEM(operand.shape, operand.dtype) for operand in operands]
        + [pltpu.SemaphoreType.DMA((len(operands),))],
        compiler_params=pltpu.CompilerParams(vmem_limit_bytes=SMALL_VMEM),
        cost_estimate=pl.CostEstimate(flops=beside, bytes_accessed=0, transcendentals=0),
    )(*(pltpu.with_memory_space_constraint(operand, pltpu.HBM) for operand in operands))


def later_pack_kernel(tick, per_expert, slices, *refs):
    tables, section_ref, enter_refs, out_ref = refs[:4], refs[4], refs[5:7], refs[7]
    pack_into(out_ref, tick, per_expert, slices, tables, arriving(section_ref, enter_refs))


def later_pack(tick, devices, per_expert, slices, routing, arrived, *entering):
    return pl.pallas_call(
        functools.partial(later_pack_kernel, tick, per_expert, slices),
        out_shape=pltpu.VMEM((devices, 4 * per_expert, arrived.shape[-1]), jnp.bfloat16),
        in_specs=[VMEM] * 7,
        out_specs=VMEM,
        compiler_params=pltpu.CompilerParams(vmem_limit_bytes=SMALL_VMEM),
    )(*routing, arrived, *entering)


def mixed_halves(tick, per_expert, slices, tables, back_ref, pairs):
    devices, block, half_width = back_ref.shape
    rows = devices * block
    back = back_ref[...].reshape(rows, half_width)
    terms = []
    for direction in range(2):
        _, weight = placing(
            tables[2 * direction], tables[2 * direction + 1], tick, direction, rows, per_expert, slices
        )
        side = half_of(rows, weight.shape[1], per_expert)
        sides = jnp.concatenate(
            [jnp.where(side == half, weight, 0.0) for half in range(2)], axis=1
        )
        high = sides.astype(jnp.bfloat16).astype(jnp.float32)
        middle = (sides - high).astype(jnp.bfloat16).astype(jnp.float32)
        terms += [sides - high - middle, middle, high]
    mixed = lax.dot_general(
        jnp.concatenate(terms, axis=1).astype(jnp.bfloat16),
        back,
        (((0,), (0,)), ((), ())),
        preferred_element_type=jnp.float32,
    )
    results = []
    for direction, halves in enumerate(pairs):
        total = jnp.concatenate([half.astype(jnp.float32) for half in halves], axis=0)
        count = total.shape[0]
        for term in range(3):
            start = (3 * direction + term) * count
            total = total + mixed[start : start + count]
        results.append(total.astype(jnp.bfloat16))
    return results


def relay_kernel(tick, per_expert, slices, *refs):
    tables, back_ref, token_refs, section_ref, next_refs = refs[:4], refs[4], refs[5:7], refs[7], refs[8:]
    half_width = back_ref.shape[2]
    section, last = lax.axis_index("section"), lax.axis_size("section") - 1
    pairs = [split_rows(tokens_ref[0]) for tokens_ref in token_refs]
    results = mixed_halves(tick, per_expert, slices, tables, back_ref, pairs)
    section_ref[...] = jnp.zeros_like(section_ref)
    for result, next_ref in zip(results, next_refs):
        count = result.shape[0] // 2
        for half in range(2):
            next_ref[:, half * half_width : (half + 1) * half_width] = result[
                half * count : (half + 1) * count
            ]

    @pl.when(section < last)
    def _():
        section_ref[jnp.minimum(section + 1, last)] = results[0]

    @pl.when(section > 0)
    def _():
        section_ref[jnp.maximum(section - 1, 0)] = results[1]


def relay(tick, per_expert, slices, routing, back, fwd, bwd):
    tokens, width = fwd.shape[-2:]
    sections = lax.axis_size("section")
    return pl.pallas_call(
        functools.partial(relay_kernel, tick, per_expert, slices),
        out_shape=[pltpu.VMEM((sections, 2 * tokens, width // 2), jnp.bfloat16)]
        + [pltpu.VMEM((tokens, width), jnp.bfloat16)] * 2,
        in_specs=[VMEM] * 7,
        out_specs=[VMEM] * 3,
        compiler_params=pltpu.CompilerParams(vmem_limit_bytes=SMALL_VMEM),
    )(*routing, back, fwd, bwd)


def finish_kernel(tick, per_expert, slices, *refs):
    tables, back_ref, section_ref, enter_refs, earlier_refs, out_refs = (
        refs[:4], refs[4], refs[5], refs[6:8], refs[8:10], refs[10:],
    )
    half_width = back_ref.shape[2]
    pairs = arriving(section_ref, enter_refs)
    results = mixed_halves(tick, per_expert, slices, tables, back_ref, pairs)
    for result, earlier_ref, out_ref in zip(results, earlier_refs, out_refs):
        count = result.shape[0] // 2
        out_ref[0, 0] = earlier_ref[...]
        for half in range(2):
            out_ref[tick, 0, :, half * half_width : (half + 1) * half_width] = result[
                half * count : (half + 1) * count
            ]


def finish(tick, per_expert, slices, routing, back, arrived, *others):
    tokens, width = others[0].shape
    return pl.pallas_call(
        functools.partial(finish_kernel, tick, per_expert, slices),
        out_shape=[jax.ShapeDtypeStruct((TICKS, 1, tokens, width), jnp.bfloat16)] * 2,
        in_specs=[VMEM] * 10,
        out_specs=[VMEM] * 2,
        compiler_params=pltpu.CompilerParams(vmem_limit_bytes=SMALL_VMEM),
    )(*routing, back, arrived, *others)


def home_of(line, slots, per_expert):
    half, direction, slot = line // (2 * slots), line // slots % 2, line % slots
    return (
        slot // per_expert * (4 * per_expert)
        + (2 * half + direction) * per_expert
        + slot % per_expert
    )


def backward_kernel(tick, rows_ref, saved_ref, w_in, w_out, fwd_rows, back_ref, saved, bwd_rows, joined, saved_sem):
    devices, block, half_width = rows_ref.shape
    per_expert = block // 4
    slots = devices * per_expert
    hidden_units = w_out.shape[0]
    rows = devices * block

    saved_copy = pltpu.make_async_copy(saved_ref.at[tick, 0, 0], saved, saved_sem)
    saved_copy.start()

    received = rows_ref[...].reshape(rows, half_width)
    line = lax.broadcasted_iota(jnp.int32, (4 * slots, rows), 0)
    row = lax.broadcasted_iota(jnp.int32, (4 * slots, rows), 1)
    pick = jnp.where(row == home_of(line, slots, per_expert), 1.0, 0.0)
    picked = exact_dot(pick, received).astype(jnp.bfloat16)
    for half in range(2):
        columns = slice(half * half_width, (half + 1) * half_width)
        start = half * 2 * slots
        fwd_rows[:, columns] = picked[start : start + slots]
        bwd_rows[:, columns] = picked[start + slots : start + 2 * slots]

    grad = lax.dot_general(
        bwd_rows[...], w_out[...], (((1,), (1,)), ((), ())), preferred_element_type=jnp.float32
    )
    saved_copy.wait()
    gate_pre = saved[:, :hidden_units]
    sigma = jax.nn.sigmoid(gate_pre)
    slope = sigma * (1.0 + gate_pre * (1.0 - sigma))
    joined[:, :hidden_units] = (grad * saved[:, hidden_units:] * slope).astype(jnp.bfloat16)
    joined[:, hidden_units:] = (grad * (gate_pre * sigma)).astype(jnp.bfloat16)
    back_ref[...] = lax.dot_general(
        joined[...], w_in[...], (((1,), (1,)), ((), ())), preferred_element_type=jnp.float32
    ).astype(jnp.bfloat16)


def lay_kernel(ahead_ref, back_ref, out_ref, parts):
    devices, block, half_width = out_ref.shape
    per_expert = block // 4
    slots = devices * per_expert
    rows = devices * block
    for half in range(2):
        columns = slice(half * half_width, (half + 1) * half_width)
        start = half * 2 * slots
        parts[start : start + slots] = ahead_ref[:, columns]
        parts[start + slots : start + 2 * slots] = back_ref[:, columns]
    row = lax.broadcasted_iota(jnp.int32, (rows, 4 * slots), 0)
    line = lax.broadcasted_iota(jnp.int32, (rows, 4 * slots), 1)
    spread = jnp.where(row == home_of(line, slots, per_expert), 1.0, 0.0)
    out_ref[...] = exact_dot(spread, parts[...]).astype(jnp.bfloat16).reshape(out_ref.shape)


def expert_step(tick, rows, saved_pre, plain, pinned):
    w_in, w_out = plain
    width, both = w_in.shape
    hidden_units = both // 2
    slots = saved_pre.shape[3]
    fwd_rows, back = pl.pallas_call(
        functools.partial(backward_kernel, tick),
        out_shape=[pltpu.VMEM((slots, width), jnp.bfloat16)] * 2,
        in_specs=[VMEM, HBM, VMEM, VMEM],
        out_specs=[VMEM] * 2,
        scratch_shapes=[
            pltpu.VMEM((slots, both), jnp.float32),
            pltpu.VMEM((slots, width), jnp.bfloat16),
            pltpu.VMEM((slots, both), jnp.bfloat16),
            pltpu.SemaphoreType.DMA,
        ],
        compiler_params=pltpu.CompilerParams(vmem_limit_bytes=EXPERT_VMEM),
        cost_estimate=pl.CostEstimate(
            flops=6 * slots * width * hidden_units, bytes_accessed=0, transcendentals=0
        ),
    )(rows, pltpu.with_memory_space_constraint(saved_pre, pltpu.HBM), *pinned)
    gate_up = jnp.dot(fwd_rows, w_in, preferred_element_type=jnp.float32)
    hidden = (jax.nn.silu(gate_up[:, :hidden_units]) * gate_up[:, hidden_units:]).astype(
        jnp.bfloat16
    )
    ahead = jnp.dot(hidden, w_out, preferred_element_type=jnp.float32).astype(jnp.bfloat16)
    return pl.pallas_call(
        lay_kernel,
        out_shape=pltpu.VMEM(rows.shape, jnp.bfloat16),
        in_specs=[VMEM] * 2,
        out_specs=VMEM,
        scratch_shapes=[pltpu.VMEM((4 * slots, width // 2), jnp.bfloat16)],
        compiler_params=pltpu.CompilerParams(vmem_limit_bytes=SMALL_VMEM),
    )(ahead, back)


def exchange(array, axis):
    return lax.all_to_all(array, axis, split_axis=0, concat_axis=0, tiled=True)


def shards(
    fwd_act,
    fwd_enter,
    bwd_grad,
    bwd_enter,
    w_in,
    w_out,
    fwd_route,
    fwd_gate,
    bwd_route,
    bwd_gate,
    saved_pre,
):
    devices = lax.axis_size("expert")
    slices = FF // w_out.shape[2]
    per_expert = saved_pre.shape[3] // devices
    routing = [
        jnp.swapaxes(table, 2, 3) for table in (fwd_route, fwd_gate, bwd_route, bwd_gate)
    ]
    beside = BESIDE * (w_in.size + w_out.size)
    plain = [w.reshape(w.shape[2:]) for w in (w_in, w_out)]
    pinned = [pltpu.with_memory_space_constraint(w, pltpu.VMEM) for w in plain]
    sent = first_pack(0, devices, per_expert, slices, routing, fwd_act, bwd_grad, beside)
    parts = expert_step(0, exchange(sent, "expert"), saved_pre, plain, pinned)
    moved, fwd_next, bwd_next = relay(
        0, per_expert, slices, routing, exchange(parts, "expert"), fwd_act, bwd_grad
    )
    arrived = exchange(moved, "section")
    sent = later_pack(1, devices, per_expert, slices, routing, arrived, fwd_enter, bwd_enter)
    parts = expert_step(1, exchange(sent, "expert"), saved_pre, plain, pinned)
    return finish(
        1, per_expert, slices, routing, exchange(parts, "expert"), arrived,
        fwd_enter, bwd_enter, fwd_next, bwd_next,
    )


def solution(mesh):
    placed = (
        P("section", "expert", None),
        P("expert", None),
        P("section", "expert", None),
        P("expert", None),
        P("section", "expert", None, None),
        P("section", "expert", None, None),
        P(None, "section", "expert", None),
        P(None, "section", "expert", None),
        P(None, "section", "expert", None),
        P(None, "section", "expert", None),
        P(None, "section", "expert", None, None),
    )
    return jax.shard_map(
        shards,
        mesh=mesh,
        in_specs=placed,
        out_specs=(P(None, "section", "expert", None), P(None, "section", "expert", None)),
        check_vma=False,
    )
```

```python
import functools

import jax
import jax.numpy as jnp
from jax import lax
from jax.experimental import pallas as pl
from jax.experimental.pallas import tpu as pltpu
from jax.sharding import PartitionSpec as P

FF = 1024
TICKS = 2
EXPERT_VMEM = 16 * 1024 * 1024
BESIDE = 2000
SMALL_VMEM = 8 * 1024 * 1024
VMEM = pl.BlockSpec(memory_space=pltpu.VMEM)
HBM = pl.BlockSpec(memory_space=pltpu.HBM)


def exact_dot(one_hot, values):
    return jnp.dot(one_hot.astype(jnp.bfloat16), values, preferred_element_type=jnp.float32)


def placing(route_ref, gate_ref, tick, direction, rows, per_expert, slices):
    route = route_ref[tick, 0]
    gate = gate_ref[tick, 0]
    top, tokens = route.shape
    block = 4 * per_expert
    row = lax.broadcasted_iota(jnp.int32, (rows, tokens), 0)
    expert = row // (block * slices)
    mine = (row // per_expert) % 2 == direction
    hit = jnp.zeros((rows, tokens), jnp.float32)
    weight = jnp.zeros((rows, tokens), jnp.float32)
    for column in range(top):
        named = route[column : column + 1, :] == expert
        hit = jnp.where(named, 1.0, hit)
        weight = jnp.where(named, gate[column : column + 1, :], weight)
    lane = lax.broadcasted_iota(jnp.int32, (rows, tokens), 1)
    rank = jnp.zeros((rows, tokens), jnp.float32)
    for token in range(tokens - 1):
        rank = rank + jnp.where(lane > token, hit[:, token : token + 1], 0.0)
    place = jnp.where(
        mine & (hit > 0.0) & (rank.astype(jnp.int32) == row % per_expert), 1.0, 0.0
    )
    return place, weight * place


def half_of(rows, width, per_expert):
    row = lax.broadcasted_iota(jnp.int32, (rows, width), 0)
    return (row // (2 * per_expert)) % 2


def whole_rows(rows_ref, index):
    block = rows_ref[index]
    count = block.shape[0] // 2
    return block[:count], block[count:]


def arriving(section_ref, enter_refs):
    section, last = lax.axis_index("section"), lax.axis_size("section") - 1
    pairs = []
    for source, edge, enter_ref in (
        (section - 1, section == 0, enter_refs[0]),
        (section + 1, section == last, enter_refs[1]),
    ):
        halves = whole_rows(section_ref, jnp.clip(source, 0, last))
        half_width = halves[0].shape[1]
        pairs.append(
            [
                jnp.where(edge, enter_ref[:, half * half_width : (half + 1) * half_width], halves[half])
                for half in range(2)
            ]
        )
    return pairs


def split_rows(rows):
    half_width = rows.shape[-1] // 2
    return [rows[:, :half_width], rows[:, half_width:]]


def pack_into(out_ref, tick, per_expert, slices, tables, pairs):
    devices, block, half_width = out_ref.shape
    rows = devices * block
    places, values = [], []
    for direction, halves in enumerate(pairs):
        place, _ = placing(
            tables[2 * direction], tables[2 * direction + 1], tick, direction, rows, per_expert, slices
        )
        side = half_of(rows, place.shape[1], per_expert)
        places += [jnp.where(side == half, place, 0.0) for half in range(2)]
        values += [value.astype(jnp.float32) for value in halves]
    total = exact_dot(
        jnp.concatenate(places, axis=1), jnp.concatenate(values, axis=0).astype(jnp.bfloat16)
    )
    out_ref[...] = total.astype(jnp.bfloat16).reshape(out_ref.shape)


def first_pack_kernel(tick, per_expert, slices, *refs):
    operands, out_ref, local, sem = refs[:6], refs[6], refs[7:13], refs[13]
    copies = [
        pltpu.make_async_copy(source, target, sem.at[index])
        for index, (source, target) in enumerate(zip(operands, local))
    ]
    for copy in copies:
        copy.start()
    for copy in copies:
        copy.wait()
    pairs = [split_rows(tokens_ref[0]) for tokens_ref in local[4:]]
    pack_into(out_ref, tick, per_expert, slices, local[:4], pairs)


def first_pack(tick, devices, per_expert, slices, routing, fwd, bwd, beside):
    operands = [*routing, fwd, bwd]
    return pl.pallas_call(
        functools.partial(first_pack_kernel, tick, per_expert, slices),
        out_shape=pltpu.VMEM((devices, 4 * per_expert, fwd.shape[-1] // 2), jnp.bfloat16),
        in_specs=[HBM] * len(operands),
        out_specs=VMEM,
        scratch_shapes=[pltpu.VMEM(operand.shape, operand.dtype) for operand in operands]
        + [pltpu.SemaphoreType.DMA((len(operands),))],
        compiler_params=pltpu.CompilerParams(vmem_limit_bytes=SMALL_VMEM),
        cost_estimate=pl.CostEstimate(flops=beside, bytes_accessed=0, transcendentals=0),
    )(*(pltpu.with_memory_space_constraint(operand, pltpu.HBM) for operand in operands))


def later_pack_kernel(tick, per_expert, slices, *refs):
    tables, section_ref, enter_refs, out_ref = refs[:4], refs[4], refs[5:7], refs[7]
    pack_into(out_ref, tick, per_expert, slices, tables, arriving(section_ref, enter_refs))


def later_pack(tick, devices, per_expert, slices, routing, arrived, *entering):
    return pl.pallas_call(
        functools.partial(later_pack_kernel, tick, per_expert, slices),
        out_shape=pltpu.VMEM((devices, 4 * per_expert, arrived.shape[-1]), jnp.bfloat16),
        in_specs=[VMEM] * 7,
        out_specs=VMEM,
        compiler_params=pltpu.CompilerParams(vmem_limit_bytes=SMALL_VMEM),
    )(*routing, arrived, *entering)


def mixed_halves(tick, per_expert, slices, tables, back_ref, pairs):
    devices, block, half_width = back_ref.shape
    rows = devices * block
    back = back_ref[...].reshape(rows, half_width)
    terms = []
    for direction in range(2):
        _, weight = placing(
            tables[2 * direction], tables[2 * direction + 1], tick, direction, rows, per_expert, slices
        )
        side = half_of(rows, weight.shape[1], per_expert)
        sides = jnp.concatenate(
            [jnp.where(side == half, weight, 0.0) for half in range(2)], axis=1
        )
        high = sides.astype(jnp.bfloat16).astype(jnp.float32)
        middle = (sides - high).astype(jnp.bfloat16).astype(jnp.float32)
        terms += [sides - high - middle, middle, high]
    mixed = lax.dot_general(
        jnp.concatenate(terms, axis=1).astype(jnp.bfloat16),
        back,
        (((0,), (0,)), ((), ())),
        preferred_element_type=jnp.float32,
    )
    results = []
    for direction, halves in enumerate(pairs):
        total = jnp.concatenate([half.astype(jnp.float32) for half in halves], axis=0)
        count = total.shape[0]
        for term in range(3):
            start = (3 * direction + term) * count
            total = total + mixed[start : start + count]
        results.append(total.astype(jnp.bfloat16))
    return results


def relay_kernel(tick, per_expert, slices, *refs):
    tables, back_ref, token_refs, section_ref, next_refs = refs[:4], refs[4], refs[5:7], refs[7], refs[8:]
    half_width = back_ref.shape[2]
    section, last = lax.axis_index("section"), lax.axis_size("section") - 1
    pairs = [split_rows(tokens_ref[0]) for tokens_ref in token_refs]
    results = mixed_halves(tick, per_expert, slices, tables, back_ref, pairs)
    section_ref[...] = jnp.zeros_like(section_ref)
    for result, next_ref in zip(results, next_refs):
        count = result.shape[0] // 2
        for half in range(2):
            next_ref[:, half * half_width : (half + 1) * half_width] = result[
                half * count : (half + 1) * count
            ]

    @pl.when(section < last)
    def _():
        section_ref[jnp.minimum(section + 1, last)] = results[0]

    @pl.when(section > 0)
    def _():
        section_ref[jnp.maximum(section - 1, 0)] = results[1]


def relay(tick, per_expert, slices, routing, back, fwd, bwd):
    tokens, width = fwd.shape[-2:]
    sections = lax.axis_size("section")
    return pl.pallas_call(
        functools.partial(relay_kernel, tick, per_expert, slices),
        out_shape=[pltpu.VMEM((sections, 2 * tokens, width // 2), jnp.bfloat16)]
        + [pltpu.VMEM((tokens, width), jnp.bfloat16)] * 2,
        in_specs=[VMEM] * 7,
        out_specs=[VMEM] * 3,
        compiler_params=pltpu.CompilerParams(vmem_limit_bytes=SMALL_VMEM),
    )(*routing, back, fwd, bwd)


def finish_kernel(tick, per_expert, slices, *refs):
    tables, back_ref, section_ref, enter_refs, earlier_refs, out_refs = (
        refs[:4], refs[4], refs[5], refs[6:8], refs[8:10], refs[10:],
    )
    half_width = back_ref.shape[2]
    pairs = arriving(section_ref, enter_refs)
    results = mixed_halves(tick, per_expert, slices, tables, back_ref, pairs)
    for result, earlier_ref, out_ref in zip(results, earlier_refs, out_refs):
        count = result.shape[0] // 2
        out_ref[0, 0] = earlier_ref[...]
        for half in range(2):
            out_ref[tick, 0, :, half * half_width : (half + 1) * half_width] = result[
                half * count : (half + 1) * count
            ]


def finish(tick, per_expert, slices, routing, back, arrived, *others):
    tokens, width = others[0].shape
    return pl.pallas_call(
        functools.partial(finish_kernel, tick, per_expert, slices),
        out_shape=[jax.ShapeDtypeStruct((TICKS, 1, tokens, width), jnp.bfloat16)] * 2,
        in_specs=[VMEM] * 10,
        out_specs=[VMEM] * 2,
        compiler_params=pltpu.CompilerParams(vmem_limit_bytes=SMALL_VMEM),
    )(*routing, back, arrived, *others)


def home_of(line, slots, per_expert):
    half, direction, slot = line // (2 * slots), line // slots % 2, line % slots
    return (
        slot // per_expert * (4 * per_expert)
        + (2 * half + direction) * per_expert
        + slot % per_expert
    )


def expert_kernel(tick, rows_ref, saved_ref, w_in, w_out, out_ref, *rest):
    saved, fwd_rows, bwd_columns, joined, parts, saved_sem = rest
    devices, block, half_width = rows_ref.shape
    per_expert = block // 4
    slots = devices * per_expert
    width, both = w_in.shape
    hidden_units = both // 2
    rows = devices * block

    saved_copy = pltpu.make_async_copy(saved_ref.at[tick, 0, 0], saved, saved_sem)
    saved_copy.start()

    received = rows_ref[...].reshape(rows, half_width)
    line = lax.broadcasted_iota(jnp.int32, (4 * slots, rows), 0)
    row = lax.broadcasted_iota(jnp.int32, (4 * slots, rows), 1)
    pick = jnp.where(row == home_of(line, slots, per_expert), 1.0, 0.0)
    picked = exact_dot(pick, received)
    for half in range(2):
        columns = slice(half * half_width, (half + 1) * half_width)
        start = half * 2 * slots
        fwd_rows[:, columns] = picked[start : start + slots].astype(jnp.bfloat16)
        bwd_columns[columns, :] = picked[start + slots : start + 2 * slots].T.astype(jnp.bfloat16)

    grad = jnp.dot(w_out[...], bwd_columns[...], preferred_element_type=jnp.float32).T
    gate_up = jnp.dot(fwd_rows[...], w_in[...], preferred_element_type=jnp.float32)
    saved_copy.wait()
    gate_pre = saved[:, :hidden_units]
    sigma = jax.nn.sigmoid(gate_pre)
    slope = sigma * (1.0 + gate_pre * (1.0 - sigma))
    joined[:hidden_units] = (grad * saved[:, hidden_units:] * slope).T.astype(jnp.bfloat16)
    joined[hidden_units:] = (grad * (gate_pre * sigma)).T.astype(jnp.bfloat16)
    gate = gate_up[:, :hidden_units]
    hidden = (gate * jax.nn.sigmoid(gate) * gate_up[:, hidden_units:]).astype(jnp.bfloat16)
    back = jnp.dot(w_in[...], joined[...], preferred_element_type=jnp.float32).T.astype(jnp.bfloat16)
    ahead = jnp.dot(hidden, w_out[...], preferred_element_type=jnp.float32).astype(jnp.bfloat16)
    for half in range(2):
        columns = slice(half * half_width, (half + 1) * half_width)
        start = half * 2 * slots
        parts[start : start + slots] = ahead[:, columns]
        parts[start + slots : start + 2 * slots] = back[:, columns]

    row = lax.broadcasted_iota(jnp.int32, (rows, 4 * slots), 0)
    line = lax.broadcasted_iota(jnp.int32, (rows, 4 * slots), 1)
    spread = jnp.where(row == home_of(line, slots, per_expert), 1.0, 0.0)
    out_ref[...] = exact_dot(spread, parts[...]).astype(jnp.bfloat16).reshape(out_ref.shape)


def expert_step(tick, rows, saved_pre, w_in, w_out):
    width, both = w_in.shape
    slots = saved_pre.shape[3]
    return pl.pallas_call(
        functools.partial(expert_kernel, tick),
        out_shape=pltpu.VMEM(rows.shape, jnp.bfloat16),
        in_specs=[VMEM, HBM, VMEM, VMEM],
        out_specs=VMEM,
        scratch_shapes=[
            pltpu.VMEM((slots, both), jnp.float32),
            pltpu.VMEM((slots, width), jnp.bfloat16),
            pltpu.VMEM((width, slots), jnp.bfloat16),
            pltpu.VMEM((both, slots), jnp.bfloat16),
            pltpu.VMEM((4 * slots, width // 2), jnp.bfloat16),
            pltpu.SemaphoreType.DMA,
        ],
        compiler_params=pltpu.CompilerParams(vmem_limit_bytes=EXPERT_VMEM),
        cost_estimate=pl.CostEstimate(
            flops=12 * slots * width * (both // 2),
            bytes_accessed=0,
            transcendentals=0,
        ),
    )(rows, pltpu.with_memory_space_constraint(saved_pre, pltpu.HBM), w_in, w_out)


def exchange(array, axis):
    return lax.all_to_all(array, axis, split_axis=0, concat_axis=0, tiled=True)


def shards(
    fwd_act,
    fwd_enter,
    bwd_grad,
    bwd_enter,
    w_in,
    w_out,
    fwd_route,
    fwd_gate,
    bwd_route,
    bwd_gate,
    saved_pre,
):
    devices = lax.axis_size("expert")
    slices = FF // w_out.shape[2]
    per_expert = saved_pre.shape[3] // devices
    routing = [
        jnp.swapaxes(table, 2, 3) for table in (fwd_route, fwd_gate, bwd_route, bwd_gate)
    ]
    beside = BESIDE * (w_in.size + w_out.size)
    w_in, w_out = (
        pltpu.with_memory_space_constraint(w.reshape(w.shape[2:]), pltpu.VMEM) for w in (w_in, w_out)
    )
    sent = first_pack(0, devices, per_expert, slices, routing, fwd_act, bwd_grad, beside)
    parts = expert_step(0, exchange(sent, "expert"), saved_pre, w_in, w_out)
    moved, fwd_next, bwd_next = relay(
        0, per_expert, slices, routing, exchange(parts, "expert"), fwd_act, bwd_grad
    )
    arrived = exchange(moved, "section")
    sent = later_pack(1, devices, per_expert, slices, routing, arrived, fwd_enter, bwd_enter)
    parts = expert_step(1, exchange(sent, "expert"), saved_pre, w_in, w_out)
    return finish(
        1, per_expert, slices, routing, exchange(parts, "expert"), arrived,
        fwd_enter, bwd_enter, fwd_next, bwd_next,
    )


def solution(mesh):
    placed = (
        P("section", "expert", None),
        P("expert", None),
        P("section", "expert", None),
        P("expert", None),
        P("section", "expert", None, None),
        P("section", "expert", None, None),
        P(None, "section", "expert", None),
        P(None, "section", "expert", None),
        P(None, "section", "expert", None),
        P(None, "section", "expert", None),
        P(None, "section", "expert", None, None),
    )
    return jax.shard_map(
        shards,
        mesh=mesh,
        in_specs=placed,
        out_specs=(P(None, "section", "expert", None), P(None, "section", "expert", None)),
        check_vma=False,
    )
```

```python
import functools

import jax
import jax.numpy as jnp
from jax import lax
from jax.experimental import pallas as pl
from jax.experimental.pallas import tpu as pltpu
from jax.sharding import PartitionSpec as P

FF = 1024
TICKS = 2
EXPERT_VMEM = 16 * 1024 * 1024
BESIDE = 2000
SMALL_VMEM = 8 * 1024 * 1024
VMEM = pl.BlockSpec(memory_space=pltpu.VMEM)
HBM = pl.BlockSpec(memory_space=pltpu.HBM)


def exact_dot(one_hot, values):
    return jnp.dot(one_hot.astype(jnp.bfloat16), values, preferred_element_type=jnp.float32)


def placing(route_ref, gate_ref, tick, direction, rows, per_expert, slices):
    route = route_ref[tick, 0]
    gate = gate_ref[tick, 0]
    top, tokens = route.shape
    block = 4 * per_expert
    row = lax.broadcasted_iota(jnp.int32, (rows, tokens), 0)
    expert = row // (block * slices)
    mine = (row // per_expert) % 2 == direction
    hit = jnp.zeros((rows, tokens), jnp.float32)
    weight = jnp.zeros((rows, tokens), jnp.float32)
    for column in range(top):
        named = route[column : column + 1, :] == expert
        hit = jnp.where(named, 1.0, hit)
        weight = jnp.where(named, gate[column : column + 1, :], weight)
    lane = lax.broadcasted_iota(jnp.int32, (rows, tokens), 1)
    rank = jnp.zeros((rows, tokens), jnp.float32)
    for token in range(tokens - 1):
        rank = rank + jnp.where(lane > token, hit[:, token : token + 1], 0.0)
    place = jnp.where(
        mine & (hit > 0.0) & (rank.astype(jnp.int32) == row % per_expert), 1.0, 0.0
    )
    return place, weight * place


def half_of(rows, width, per_expert):
    row = lax.broadcasted_iota(jnp.int32, (rows, width), 0)
    return (row // (2 * per_expert)) % 2


def whole_rows(rows_ref, index):
    block = rows_ref[index]
    count = block.shape[0] // 2
    return block[:count], block[count:]


def arriving(section_ref, enter_refs):
    section, last = lax.axis_index("section"), lax.axis_size("section") - 1
    pairs = []
    for source, edge, enter_ref in (
        (section - 1, section == 0, enter_refs[0]),
        (section + 1, section == last, enter_refs[1]),
    ):
        halves = whole_rows(section_ref, jnp.clip(source, 0, last))
        half_width = halves[0].shape[1]
        pairs.append(
            [
                jnp.where(edge, enter_ref[:, half * half_width : (half + 1) * half_width], halves[half])
                for half in range(2)
            ]
        )
    return pairs


def split_rows(rows):
    half_width = rows.shape[-1] // 2
    return [rows[:, :half_width], rows[:, half_width:]]


def pack_into(out_ref, tick, per_expert, slices, tables, pairs):
    devices, block, half_width = out_ref.shape
    rows = devices * block
    places = []
    for direction in range(2):
        place, _ = placing(
            tables[2 * direction], tables[2 * direction + 1], tick, direction, rows, per_expert, slices
        )
        side = half_of(rows, place.shape[1], per_expert)
        places += [jnp.where(side == half, place, 0.0) for half in range(2)]
    values = [half.astype(jnp.float32) for halves in pairs() for half in halves]
    total = exact_dot(
        jnp.concatenate(places, axis=1), jnp.concatenate(values, axis=0).astype(jnp.bfloat16)
    )
    out_ref[...] = total.astype(jnp.bfloat16).reshape(out_ref.shape)


def first_pack_kernel(tick, per_expert, slices, *refs):
    operands, out_ref, local, sem = refs[:6], refs[6], refs[7:13], refs[13]
    copies = [
        pltpu.make_async_copy(source, target, sem.at[index])
        for index, (source, target) in enumerate(zip(operands, local))
    ]
    for copy in copies:
        copy.start()
    for copy in copies[:4]:
        copy.wait()

    def pairs():
        for copy in copies[4:]:
            copy.wait()
        return [split_rows(tokens_ref[0]) for tokens_ref in local[4:]]

    pack_into(out_ref, tick, per_expert, slices, local[:4], pairs)


def first_pack(tick, devices, per_expert, slices, routing, fwd, bwd, beside):
    operands = [*routing, fwd, bwd]
    return pl.pallas_call(
        functools.partial(first_pack_kernel, tick, per_expert, slices),
        out_shape=pltpu.VMEM((devices, 4 * per_expert, fwd.shape[-1] // 2), jnp.bfloat16),
        in_specs=[HBM] * len(operands),
        out_specs=VMEM,
        scratch_shapes=[pltpu.VMEM(operand.shape, operand.dtype) for operand in operands]
        + [pltpu.SemaphoreType.DMA((len(operands),))],
        compiler_params=pltpu.CompilerParams(vmem_limit_bytes=SMALL_VMEM),
        cost_estimate=pl.CostEstimate(flops=beside, bytes_accessed=0, transcendentals=0),
    )(*(pltpu.with_memory_space_constraint(operand, pltpu.HBM) for operand in operands))


def later_pack_kernel(tick, per_expert, slices, *refs):
    tables, section_ref, enter_refs, out_ref = refs[:4], refs[4], refs[5:7], refs[7]
    pack_into(out_ref, tick, per_expert, slices, tables, lambda: arriving(section_ref, enter_refs))


def later_pack(tick, devices, per_expert, slices, routing, arrived, *entering):
    return pl.pallas_call(
        functools.partial(later_pack_kernel, tick, per_expert, slices),
        out_shape=pltpu.VMEM((devices, 4 * per_expert, arrived.shape[-1]), jnp.bfloat16),
        in_specs=[VMEM] * 7,
        out_specs=VMEM,
        compiler_params=pltpu.CompilerParams(vmem_limit_bytes=SMALL_VMEM),
    )(*routing, arrived, *entering)


def mixed_halves(tick, per_expert, slices, tables, back_ref, pairs):
    devices, block, half_width = back_ref.shape
    rows = devices * block
    back = back_ref[...].reshape(rows, half_width)
    terms = []
    for direction in range(2):
        _, weight = placing(
            tables[2 * direction], tables[2 * direction + 1], tick, direction, rows, per_expert, slices
        )
        side = half_of(rows, weight.shape[1], per_expert)
        sides = jnp.concatenate(
            [jnp.where(side == half, weight, 0.0) for half in range(2)], axis=1
        )
        high = sides.astype(jnp.bfloat16).astype(jnp.float32)
        middle = (sides - high).astype(jnp.bfloat16).astype(jnp.float32)
        terms += [sides - high - middle, middle, high]
    mixed = lax.dot_general(
        jnp.concatenate(terms, axis=1).astype(jnp.bfloat16),
        back,
        (((0,), (0,)), ((), ())),
        preferred_element_type=jnp.float32,
    )
    results = []
    for direction, halves in enumerate(pairs):
        total = jnp.concatenate([half.astype(jnp.float32) for half in halves], axis=0)
        count = total.shape[0]
        for term in range(3):
            start = (3 * direction + term) * count
            total = total + mixed[start : start + count]
        results.append(total.astype(jnp.bfloat16))
    return results


def relay_kernel(tick, per_expert, slices, *refs):
    tables, back_ref, token_refs, section_ref, next_refs = refs[:4], refs[4], refs[5:7], refs[7], refs[8:]
    half_width = back_ref.shape[2]
    section, last = lax.axis_index("section"), lax.axis_size("section") - 1
    pairs = [split_rows(tokens_ref[0]) for tokens_ref in token_refs]
    results = mixed_halves(tick, per_expert, slices, tables, back_ref, pairs)
    section_ref[...] = jnp.zeros_like(section_ref)
    for result, next_ref in zip(results, next_refs):
        count = result.shape[0] // 2
        for half in range(2):
            next_ref[:, half * half_width : (half + 1) * half_width] = result[
                half * count : (half + 1) * count
            ]

    @pl.when(section < last)
    def _():
        section_ref[jnp.minimum(section + 1, last)] = results[0]

    @pl.when(section > 0)
    def _():
        section_ref[jnp.maximum(section - 1, 0)] = results[1]


def relay(tick, per_expert, slices, routing, back, fwd, bwd):
    tokens, width = fwd.shape[-2:]
    sections = lax.axis_size("section")
    return pl.pallas_call(
        functools.partial(relay_kernel, tick, per_expert, slices),
        out_shape=[pltpu.VMEM((sections, 2 * tokens, width // 2), jnp.bfloat16)]
        + [pltpu.VMEM((tokens, width), jnp.bfloat16)] * 2,
        in_specs=[VMEM] * 7,
        out_specs=[VMEM] * 3,
        compiler_params=pltpu.CompilerParams(vmem_limit_bytes=SMALL_VMEM),
    )(*routing, back, fwd, bwd)


def finish_kernel(tick, per_expert, slices, *refs):
    tables, back_ref, section_ref, enter_refs, earlier_refs, out_refs = (
        refs[:4], refs[4], refs[5], refs[6:8], refs[8:10], refs[10:],
    )
    half_width = back_ref.shape[2]
    pairs = arriving(section_ref, enter_refs)
    results = mixed_halves(tick, per_expert, slices, tables, back_ref, pairs)
    for result, earlier_ref, out_ref in zip(results, earlier_refs, out_refs):
        count = result.shape[0] // 2
        out_ref[0, 0] = earlier_ref[...]
        for half in range(2):
            out_ref[tick, 0, :, half * half_width : (half + 1) * half_width] = result[
                half * count : (half + 1) * count
            ]


def finish(tick, per_expert, slices, routing, back, arrived, *others):
    tokens, width = others[0].shape
    return pl.pallas_call(
        functools.partial(finish_kernel, tick, per_expert, slices),
        out_shape=[jax.ShapeDtypeStruct((TICKS, 1, tokens, width), jnp.bfloat16)] * 2,
        in_specs=[VMEM] * 10,
        out_specs=[VMEM] * 2,
        compiler_params=pltpu.CompilerParams(vmem_limit_bytes=SMALL_VMEM),
    )(*routing, back, arrived, *others)


def home_of(line, slots, per_expert):
    half, direction, slot = line // (2 * slots), line // slots % 2, line % slots
    return (
        slot // per_expert * (4 * per_expert)
        + (2 * half + direction) * per_expert
        + slot % per_expert
    )


def expert_kernel(tick, rows_ref, saved_ref, w_in, w_out, out_ref, *rest):
    slot_rows, joined, parts = rest
    devices, block, half_width = rows_ref.shape
    per_expert = block // 4
    slots = devices * per_expert
    width, both = w_in.shape
    hidden_units = both // 2
    rows = devices * block

    received = rows_ref[...].reshape(rows, half_width)
    line = lax.broadcasted_iota(jnp.int32, (4 * slots, rows), 0)
    row = lax.broadcasted_iota(jnp.int32, (4 * slots, rows), 1)
    pick = jnp.where(row == home_of(line, slots, per_expert), 1.0, 0.0)
    picked = exact_dot(pick, received).astype(jnp.bfloat16)
    for half in range(2):
        slot_rows[:, half * half_width : (half + 1) * half_width] = picked[
            half * 2 * slots : (half + 1) * 2 * slots
        ]

    grad = lax.dot_general(
        slot_rows[slots:],
        w_out[...],
        (((1,), (1,)), ((), ())),
        preferred_element_type=jnp.float32,
    )
    gate_up = jnp.dot(slot_rows[:slots], w_in[...], preferred_element_type=jnp.float32)
    gate_pre = saved_ref[tick, 0, 0, :, :hidden_units]
    sigma = jax.nn.sigmoid(gate_pre)
    slope = sigma * (1.0 + gate_pre * (1.0 - sigma))
    joined[:, :hidden_units] = (grad * saved_ref[tick, 0, 0, :, hidden_units:] * slope).astype(jnp.bfloat16)
    joined[:, hidden_units:] = (grad * (gate_pre * sigma)).astype(jnp.bfloat16)
    gate = gate_up[:, :hidden_units]
    hidden = (gate * jax.nn.sigmoid(gate) * gate_up[:, hidden_units:]).astype(jnp.bfloat16)
    back = lax.dot_general(
        joined[...], w_in[...], (((1,), (1,)), ((), ())), preferred_element_type=jnp.float32
    ).astype(jnp.bfloat16)
    ahead = jnp.dot(hidden, w_out[...], preferred_element_type=jnp.float32).astype(jnp.bfloat16)
    for half in range(2):
        columns = slice(half * half_width, (half + 1) * half_width)
        start = half * 2 * slots
        parts[start : start + slots] = ahead[:, columns]
        parts[start + slots : start + 2 * slots] = back[:, columns]

    row = lax.broadcasted_iota(jnp.int32, (rows, 4 * slots), 0)
    line = lax.broadcasted_iota(jnp.int32, (rows, 4 * slots), 1)
    spread = jnp.where(row == home_of(line, slots, per_expert), 1.0, 0.0)
    out_ref[...] = exact_dot(spread, parts[...]).astype(jnp.bfloat16).reshape(out_ref.shape)


def expert_step(tick, rows, saved_pre, w_in, w_out):
    width, both = w_in.shape
    slots = saved_pre.shape[3]
    return pl.pallas_call(
        functools.partial(expert_kernel, tick),
        out_shape=pltpu.VMEM(rows.shape, jnp.bfloat16),
        in_specs=[VMEM] * 4,
        out_specs=VMEM,
        scratch_shapes=[
            pltpu.VMEM((2 * slots, width), jnp.bfloat16),
            pltpu.VMEM((slots, both), jnp.bfloat16),
            pltpu.VMEM((4 * slots, width // 2), jnp.bfloat16),
        ],
        compiler_params=pltpu.CompilerParams(vmem_limit_bytes=EXPERT_VMEM),
        cost_estimate=pl.CostEstimate(
            flops=12 * slots * width * (both // 2),
            bytes_accessed=0,
            transcendentals=0,
        ),
    )(rows, saved_pre, w_in, w_out)


def exchange(array, axis):
    return lax.all_to_all(array, axis, split_axis=0, concat_axis=0, tiled=True)


def shards(
    fwd_act,
    fwd_enter,
    bwd_grad,
    bwd_enter,
    w_in,
    w_out,
    fwd_route,
    fwd_gate,
    bwd_route,
    bwd_gate,
    saved_pre,
):
    devices = lax.axis_size("expert")
    slices = FF // w_out.shape[2]
    per_expert = saved_pre.shape[3] // devices
    routing = [
        jnp.swapaxes(table, 2, 3) for table in (fwd_route, fwd_gate, bwd_route, bwd_gate)
    ]
    beside = BESIDE * (w_in.size + w_out.size)
    w_in, w_out = (
        pltpu.with_memory_space_constraint(w.reshape(w.shape[2:]), pltpu.VMEM) for w in (w_in, w_out)
    )
    saved_pre = pltpu.with_memory_space_constraint(saved_pre, pltpu.VMEM)
    sent = first_pack(0, devices, per_expert, slices, routing, fwd_act, bwd_grad, beside)
    parts = expert_step(0, exchange(sent, "expert"), saved_pre, w_in, w_out)
    moved, fwd_next, bwd_next = relay(
        0, per_expert, slices, routing, exchange(parts, "expert"), fwd_act, bwd_grad
    )
    arrived = exchange(moved, "section")
    sent = later_pack(1, devices, per_expert, slices, routing, arrived, fwd_enter, bwd_enter)
    parts = expert_step(1, exchange(sent, "expert"), saved_pre, w_in, w_out)
    return finish(
        1, per_expert, slices, routing, exchange(parts, "expert"), arrived,
        fwd_enter, bwd_enter, fwd_next, bwd_next,
    )


def solution(mesh):
    placed = (
        P("section", "expert", None),
        P("expert", None),
        P("section", "expert", None),
        P("expert", None),
        P("section", "expert", None, None),
        P("section", "expert", None, None),
        P(None, "section", "expert", None),
        P(None, "section", "expert", None),
        P(None, "section", "expert", None),
        P(None, "section", "expert", None),
        P(None, "section", "expert", None, None),
    )
    return jax.shard_map(
        shards,
        mesh=mesh,
        in_specs=placed,
        out_specs=(P(None, "section", "expert", None), P(None, "section", "expert", None)),
        check_vma=False,
    )
```

```python
import functools

import jax
import jax.numpy as jnp
from jax import lax
from jax.experimental import pallas as pl
from jax.experimental.pallas import tpu as pltpu
from jax.sharding import PartitionSpec as P

FF = 1024
TICKS = 2
EXPERT_VMEM = 16 * 1024 * 1024
BESIDE = 2000
SMALL_VMEM = 8 * 1024 * 1024
VMEM = pl.BlockSpec(memory_space=pltpu.VMEM)
HBM = pl.BlockSpec(memory_space=pltpu.HBM)


def exact_dot(one_hot, values):
    return jnp.dot(one_hot.astype(jnp.bfloat16), values, preferred_element_type=jnp.float32)


def placing(route_ref, gate_ref, tick, direction, rows, per_expert, slices):
    route = route_ref[tick, 0]
    gate = gate_ref[tick, 0]
    top, tokens = route.shape
    block = 4 * per_expert
    row = lax.broadcasted_iota(jnp.int32, (rows, tokens), 0)
    expert = row // (block * slices)
    mine = (row // per_expert) % 2 == direction
    hit = jnp.zeros((rows, tokens), jnp.float32)
    weight = jnp.zeros((rows, tokens), jnp.float32)
    for column in range(top):
        named = route[column : column + 1, :] == expert
        hit = jnp.where(named, 1.0, hit)
        weight = jnp.where(named, gate[column : column + 1, :], weight)
    lane = lax.broadcasted_iota(jnp.int32, (rows, tokens), 1)
    rank = jnp.zeros((rows, tokens), jnp.float32)
    for token in range(tokens - 1):
        rank = rank + jnp.where(lane > token, hit[:, token : token + 1], 0.0)
    place = jnp.where(
        mine & (hit > 0.0) & (rank.astype(jnp.int32) == row % per_expert), 1.0, 0.0
    )
    return place, weight * place


def half_of(rows, width, per_expert):
    row = lax.broadcasted_iota(jnp.int32, (rows, width), 0)
    return (row // (2 * per_expert)) % 2


def whole_rows(rows_ref, index):
    block = rows_ref[index]
    count = block.shape[0] // 2
    return block[:count], block[count:]


def arriving(section_ref, enter_refs):
    section, last = lax.axis_index("section"), lax.axis_size("section") - 1
    pairs = []
    for source, edge, enter_ref in (
        (section - 1, section == 0, enter_refs[0]),
        (section + 1, section == last, enter_refs[1]),
    ):
        halves = whole_rows(section_ref, jnp.clip(source, 0, last))
        half_width = halves[0].shape[1]
        pairs.append(
            [
                jnp.where(edge, enter_ref[:, half * half_width : (half + 1) * half_width], halves[half])
                for half in range(2)
            ]
        )
    return pairs


def split_rows(rows):
    half_width = rows.shape[-1] // 2
    return [rows[:, :half_width], rows[:, half_width:]]


def pack_into(out_ref, tick, per_expert, slices, tables, pairs):
    devices, block, half_width = out_ref.shape
    rows = devices * block
    places = []
    for direction in range(2):
        place, _ = placing(
            tables[2 * direction], tables[2 * direction + 1], tick, direction, rows, per_expert, slices
        )
        side = half_of(rows, place.shape[1], per_expert)
        places += [jnp.where(side == half, place, 0.0) for half in range(2)]
    values = [half.astype(jnp.float32) for halves in pairs() for half in halves]
    total = exact_dot(
        jnp.concatenate(places, axis=1), jnp.concatenate(values, axis=0).astype(jnp.bfloat16)
    )
    out_ref[...] = total.astype(jnp.bfloat16).reshape(out_ref.shape)


def first_pack_kernel(tick, per_expert, slices, *refs):
    operands, out_ref, local, sem = refs[:6], refs[6], refs[7:13], refs[13]
    copies = [
        pltpu.make_async_copy(source, target, sem.at[index])
        for index, (source, target) in enumerate(zip(operands, local))
    ]
    for copy in copies:
        copy.start()
    for copy in copies[:4]:
        copy.wait()

    def pairs():
        for copy in copies[4:]:
            copy.wait()
        return [split_rows(tokens_ref[0]) for tokens_ref in local[4:]]

    pack_into(out_ref, tick, per_expert, slices, local[:4], pairs)


def first_pack(tick, devices, per_expert, slices, routing, fwd, bwd, beside):
    operands = [*routing, fwd, bwd]
    return pl.pallas_call(
        functools.partial(first_pack_kernel, tick, per_expert, slices),
        out_shape=pltpu.VMEM((devices, 4 * per_expert, fwd.shape[-1] // 2), jnp.bfloat16),
        in_specs=[HBM] * len(operands),
        out_specs=VMEM,
        scratch_shapes=[pltpu.VMEM(operand.shape, operand.dtype) for operand in operands]
        + [pltpu.SemaphoreType.DMA((len(operands),))],
        compiler_params=pltpu.CompilerParams(vmem_limit_bytes=SMALL_VMEM),
        cost_estimate=pl.CostEstimate(flops=beside, bytes_accessed=0, transcendentals=0),
    )(*(pltpu.with_memory_space_constraint(operand, pltpu.HBM) for operand in operands))


def later_pack_kernel(tick, per_expert, slices, *refs):
    tables, section_ref, enter_refs, out_ref = refs[:4], refs[4], refs[5:7], refs[7]
    pack_into(out_ref, tick, per_expert, slices, tables, lambda: arriving(section_ref, enter_refs))


def later_pack(tick, devices, per_expert, slices, routing, arrived, *entering):
    return pl.pallas_call(
        functools.partial(later_pack_kernel, tick, per_expert, slices),
        out_shape=pltpu.VMEM((devices, 4 * per_expert, arrived.shape[-1]), jnp.bfloat16),
        in_specs=[VMEM] * 7,
        out_specs=VMEM,
        compiler_params=pltpu.CompilerParams(vmem_limit_bytes=SMALL_VMEM),
    )(*routing, arrived, *entering)


def mixed_halves(tick, per_expert, slices, tables, back_ref, pairs):
    devices, block, half_width = back_ref.shape
    rows = devices * block
    back = back_ref[...].reshape(rows, half_width)
    terms = []
    for direction in range(2):
        _, weight = placing(
            tables[2 * direction], tables[2 * direction + 1], tick, direction, rows, per_expert, slices
        )
        side = half_of(rows, weight.shape[1], per_expert)
        sides = jnp.concatenate(
            [jnp.where(side == half, weight, 0.0) for half in range(2)], axis=1
        )
        high = sides.astype(jnp.bfloat16).astype(jnp.float32)
        middle = (sides - high).astype(jnp.bfloat16).astype(jnp.float32)
        terms += [sides - high - middle, middle, high]
    mixed = lax.dot_general(
        jnp.concatenate(terms, axis=1).astype(jnp.bfloat16),
        back,
        (((0,), (0,)), ((), ())),
        preferred_element_type=jnp.float32,
    )
    results = []
    for direction, halves in enumerate(pairs):
        total = jnp.concatenate([half.astype(jnp.float32) for half in halves], axis=0)
        count = total.shape[0]
        for term in range(3):
            start = (3 * direction + term) * count
            total = total + mixed[start : start + count]
        results.append(total.astype(jnp.bfloat16))
    return results


def relay_kernel(tick, per_expert, slices, *refs):
    tables, back_ref, token_refs, section_ref, next_refs = refs[:4], refs[4], refs[5:7], refs[7], refs[8:]
    half_width = back_ref.shape[2]
    section, last = lax.axis_index("section"), lax.axis_size("section") - 1
    pairs = [split_rows(tokens_ref[0]) for tokens_ref in token_refs]
    results = mixed_halves(tick, per_expert, slices, tables, back_ref, pairs)
    section_ref[...] = jnp.zeros_like(section_ref)
    for result, next_ref in zip(results, next_refs):
        count = result.shape[0] // 2
        for half in range(2):
            next_ref[:, half * half_width : (half + 1) * half_width] = result[
                half * count : (half + 1) * count
            ]

    @pl.when(section < last)
    def _():
        section_ref[jnp.minimum(section + 1, last)] = results[0]

    @pl.when(section > 0)
    def _():
        section_ref[jnp.maximum(section - 1, 0)] = results[1]


def relay(tick, per_expert, slices, routing, back, fwd, bwd):
    tokens, width = fwd.shape[-2:]
    sections = lax.axis_size("section")
    return pl.pallas_call(
        functools.partial(relay_kernel, tick, per_expert, slices),
        out_shape=[pltpu.VMEM((sections, 2 * tokens, width // 2), jnp.bfloat16)]
        + [pltpu.VMEM((tokens, width), jnp.bfloat16)] * 2,
        in_specs=[VMEM] * 7,
        out_specs=[VMEM] * 3,
        compiler_params=pltpu.CompilerParams(vmem_limit_bytes=SMALL_VMEM),
    )(*routing, back, fwd, bwd)


def finish_kernel(tick, per_expert, slices, *refs):
    tables, back_ref, section_ref, enter_refs, earlier_refs, out_refs = (
        refs[:4], refs[4], refs[5], refs[6:8], refs[8:10], refs[10:],
    )
    half_width = back_ref.shape[2]
    pairs = arriving(section_ref, enter_refs)
    results = mixed_halves(tick, per_expert, slices, tables, back_ref, pairs)
    for result, earlier_ref, out_ref in zip(results, earlier_refs, out_refs):
        count = result.shape[0] // 2
        out_ref[0, 0] = earlier_ref[...]
        for half in range(2):
            out_ref[tick, 0, :, half * half_width : (half + 1) * half_width] = result[
                half * count : (half + 1) * count
            ]


def finish(tick, per_expert, slices, routing, back, arrived, *others):
    tokens, width = others[0].shape
    return pl.pallas_call(
        functools.partial(finish_kernel, tick, per_expert, slices),
        out_shape=[jax.ShapeDtypeStruct((TICKS, 1, tokens, width), jnp.bfloat16)] * 2,
        in_specs=[VMEM] * 10,
        out_specs=[VMEM] * 2,
        compiler_params=pltpu.CompilerParams(vmem_limit_bytes=SMALL_VMEM),
    )(*routing, back, arrived, *others)


def home_of(line, slots, per_expert):
    half, direction, slot = line // (2 * slots), line // slots % 2, line % slots
    return (
        slot // per_expert * (4 * per_expert)
        + (2 * half + direction) * per_expert
        + slot % per_expert
    )


def expert_kernel(tick, rows_ref, saved_ref, w_in, w_out, out_ref):
    devices, block, half_width = rows_ref.shape
    per_expert = block // 4
    slots = devices * per_expert
    width, both = w_in.shape
    hidden_units = both // 2
    rows = devices * block

    received = rows_ref[...].reshape(rows, half_width)
    line = lax.broadcasted_iota(jnp.int32, (4 * slots, rows), 0)
    row = lax.broadcasted_iota(jnp.int32, (4 * slots, rows), 1)
    pick = jnp.where(row == home_of(line, slots, per_expert), 1.0, 0.0)
    picked = exact_dot(pick, received).astype(jnp.bfloat16)
    slot_rows = jnp.concatenate([picked[: 2 * slots], picked[2 * slots :]], axis=1)

    grad = lax.dot_general(
        slot_rows[slots:],
        w_out[...],
        (((1,), (1,)), ((), ())),
        preferred_element_type=jnp.float32,
    )
    gate_up = jnp.dot(slot_rows[:slots], w_in[...], preferred_element_type=jnp.float32)
    gate_pre = saved_ref[tick, 0, 0, :, :hidden_units]
    sigma = jax.nn.sigmoid(gate_pre)
    slope = sigma * (1.0 + gate_pre * (1.0 - sigma))
    joined_gate = (grad * saved_ref[tick, 0, 0, :, hidden_units:] * slope).astype(jnp.bfloat16)
    joined_up = (grad * (gate_pre * sigma)).astype(jnp.bfloat16)
    joined = jnp.concatenate([joined_gate, joined_up], axis=1)
    gate = gate_up[:, :hidden_units]
    hidden = (gate * jax.nn.sigmoid(gate) * gate_up[:, hidden_units:]).astype(jnp.bfloat16)
    back = lax.dot_general(
        joined, w_in[...], (((1,), (1,)), ((), ())), preferred_element_type=jnp.float32
    ).astype(jnp.bfloat16)
    ahead = jnp.dot(hidden, w_out[...], preferred_element_type=jnp.float32).astype(jnp.bfloat16)
    parts = jnp.concatenate(
        [ahead[:, :half_width], back[:, :half_width], ahead[:, half_width:], back[:, half_width:]],
        axis=0,
    )

    row = lax.broadcasted_iota(jnp.int32, (rows, 4 * slots), 0)
    line = lax.broadcasted_iota(jnp.int32, (rows, 4 * slots), 1)
    spread = jnp.where(row == home_of(line, slots, per_expert), 1.0, 0.0)
    out_ref[...] = exact_dot(spread, parts).astype(jnp.bfloat16).reshape(out_ref.shape)


def expert_step(tick, rows, saved_pre, w_in, w_out):
    width, both = w_in.shape
    slots = saved_pre.shape[3]
    return pl.pallas_call(
        functools.partial(expert_kernel, tick),
        out_shape=pltpu.VMEM(rows.shape, jnp.bfloat16),
        in_specs=[VMEM] * 4,
        out_specs=VMEM,
        compiler_params=pltpu.CompilerParams(vmem_limit_bytes=EXPERT_VMEM),
        cost_estimate=pl.CostEstimate(
            flops=12 * slots * width * (both // 2),
            bytes_accessed=0,
            transcendentals=0,
        ),
    )(rows, saved_pre, w_in, w_out)


def exchange(array, axis):
    return lax.all_to_all(array, axis, split_axis=0, concat_axis=0, tiled=True)


def shards(
    fwd_act,
    fwd_enter,
    bwd_grad,
    bwd_enter,
    w_in,
    w_out,
    fwd_route,
    fwd_gate,
    bwd_route,
    bwd_gate,
    saved_pre,
):
    devices = lax.axis_size("expert")
    slices = FF // w_out.shape[2]
    per_expert = saved_pre.shape[3] // devices
    routing = [
        jnp.swapaxes(table, 2, 3) for table in (fwd_route, fwd_gate, bwd_route, bwd_gate)
    ]
    beside = BESIDE * (w_in.size + w_out.size)
    w_in, w_out = (
        pltpu.with_memory_space_constraint(w.reshape(w.shape[2:]), pltpu.VMEM) for w in (w_in, w_out)
    )
    saved_pre = pltpu.with_memory_space_constraint(saved_pre, pltpu.VMEM)
    sent = first_pack(0, devices, per_expert, slices, routing, fwd_act, bwd_grad, beside)
    parts = expert_step(0, exchange(sent, "expert"), saved_pre, w_in, w_out)
    moved, fwd_next, bwd_next = relay(
        0, per_expert, slices, routing, exchange(parts, "expert"), fwd_act, bwd_grad
    )
    arrived = exchange(moved, "section")
    sent = later_pack(1, devices, per_expert, slices, routing, arrived, fwd_enter, bwd_enter)
    parts = expert_step(1, exchange(sent, "expert"), saved_pre, w_in, w_out)
    return finish(
        1, per_expert, slices, routing, exchange(parts, "expert"), arrived,
        fwd_enter, bwd_enter, fwd_next, bwd_next,
    )


def solution(mesh):
    placed = (
        P("section", "expert", None),
        P("expert", None),
        P("section", "expert", None),
        P("expert", None),
        P("section", "expert", None, None),
        P("section", "expert", None, None),
        P(None, "section", "expert", None),
        P(None, "section", "expert", None),
        P(None, "section", "expert", None),
        P(None, "section", "expert", None),
        P(None, "section", "expert", None, None),
    )
    return jax.shard_map(
        shards,
        mesh=mesh,
        in_specs=placed,
        out_specs=(P(None, "section", "expert", None), P(None, "section", "expert", None)),
        check_vma=False,
    )
```

```python
import functools

import jax
import jax.numpy as jnp
from jax import lax
from jax.experimental import pallas as pl
from jax.experimental.pallas import tpu as pltpu
from jax.sharding import PartitionSpec as P

FF = 1024
TICKS = 2
EXPERT_VMEM = 16 * 1024 * 1024
BESIDE = 2000
SMALL_VMEM = 8 * 1024 * 1024
VMEM = pl.BlockSpec(memory_space=pltpu.VMEM)
HBM = pl.BlockSpec(memory_space=pltpu.HBM)


def exact_dot(one_hot, values):
    return jnp.dot(one_hot.astype(jnp.bfloat16), values, preferred_element_type=jnp.float32)


def placing(route_ref, gate_ref, tick, direction, rows, per_expert, slices):
    route = route_ref[tick, 0]
    gate = gate_ref[tick, 0]
    top, tokens = route.shape
    block = 4 * per_expert
    row = lax.broadcasted_iota(jnp.int32, (rows, tokens), 0)
    expert = row // (block * slices)
    mine = (row // per_expert) % 2 == direction
    hit = jnp.zeros((rows, tokens), jnp.float32)
    weight = jnp.zeros((rows, tokens), jnp.float32)
    for column in range(top):
        named = route[column : column + 1, :] == expert
        hit = jnp.where(named, 1.0, hit)
        weight = jnp.where(named, gate[column : column + 1, :], weight)
    lane = lax.broadcasted_iota(jnp.int32, (rows, tokens), 1)
    rank = jnp.zeros((rows, tokens), jnp.float32)
    for token in range(tokens - 1):
        rank = rank + jnp.where(lane > token, hit[:, token : token + 1], 0.0)
    place = jnp.where(
        mine & (hit > 0.0) & (rank.astype(jnp.int32) == row % per_expert), 1.0, 0.0
    )
    return place, weight * place


def half_of(rows, width, per_expert):
    row = lax.broadcasted_iota(jnp.int32, (rows, width), 0)
    return (row // (2 * per_expert)) % 2


def whole_rows(rows_ref, index):
    block = rows_ref[index]
    count = block.shape[0] // 2
    return block[:count], block[count:]


def arriving(section_ref, enter_refs):
    section, last = lax.axis_index("section"), lax.axis_size("section") - 1
    pairs = []
    for source, edge, enter_ref in (
        (section - 1, section == 0, enter_refs[0]),
        (section + 1, section == last, enter_refs[1]),
    ):
        halves = whole_rows(section_ref, jnp.clip(source, 0, last))
        half_width = halves[0].shape[1]
        pairs.append(
            [
                jnp.where(edge, enter_ref[:, half * half_width : (half + 1) * half_width], halves[half])
                for half in range(2)
            ]
        )
    return pairs


def split_rows(rows):
    half_width = rows.shape[-1] // 2
    return [rows[:, :half_width], rows[:, half_width:]]


def pack_into(out_ref, tick, per_expert, slices, tables, pairs):
    devices, block, half_width = out_ref.shape
    rows = devices * block
    places = []
    for direction in range(2):
        place, _ = placing(
            tables[2 * direction], tables[2 * direction + 1], tick, direction, rows, per_expert, slices
        )
        side = half_of(rows, place.shape[1], per_expert)
        places += [jnp.where(side == half, place, 0.0) for half in range(2)]
    values = [half.astype(jnp.float32) for halves in pairs() for half in halves]
    total = exact_dot(
        jnp.concatenate(places, axis=1), jnp.concatenate(values, axis=0).astype(jnp.bfloat16)
    )
    out_ref[...] = total.astype(jnp.bfloat16).reshape(out_ref.shape)


def first_pack_kernel(tick, per_expert, slices, *refs):
    operands, out_ref, local, sem = refs[:6], refs[6], refs[7:13], refs[13]
    copies = [
        pltpu.make_async_copy(source, target, sem.at[index])
        for index, (source, target) in enumerate(zip(operands, local))
    ]
    for copy in copies:
        copy.start()
    for copy in copies[:4]:
        copy.wait()

    def pairs():
        for copy in copies[4:]:
            copy.wait()
        return [split_rows(tokens_ref[0]) for tokens_ref in local[4:]]

    pack_into(out_ref, tick, per_expert, slices, local[:4], pairs)


def first_pack(tick, devices, per_expert, slices, routing, fwd, bwd, beside):
    operands = [*routing, fwd, bwd]
    return pl.pallas_call(
        functools.partial(first_pack_kernel, tick, per_expert, slices),
        out_shape=pltpu.VMEM((devices, 4 * per_expert, fwd.shape[-1] // 2), jnp.bfloat16),
        in_specs=[HBM] * len(operands),
        out_specs=VMEM,
        scratch_shapes=[pltpu.VMEM(operand.shape, operand.dtype) for operand in operands]
        + [pltpu.SemaphoreType.DMA((len(operands),))],
        compiler_params=pltpu.CompilerParams(vmem_limit_bytes=SMALL_VMEM),
        cost_estimate=pl.CostEstimate(flops=beside, bytes_accessed=0, transcendentals=0),
    )(*(pltpu.with_memory_space_constraint(operand, pltpu.HBM) for operand in operands))


def later_pack_kernel(tick, per_expert, slices, *refs):
    tables, section_ref, enter_refs, out_ref = refs[:4], refs[4], refs[5:7], refs[7]
    pack_into(out_ref, tick, per_expert, slices, tables, lambda: arriving(section_ref, enter_refs))


def later_pack(tick, devices, per_expert, slices, routing, arrived, *entering):
    return pl.pallas_call(
        functools.partial(later_pack_kernel, tick, per_expert, slices),
        out_shape=pltpu.VMEM((devices, 4 * per_expert, arrived.shape[-1]), jnp.bfloat16),
        in_specs=[VMEM] * 7,
        out_specs=VMEM,
        compiler_params=pltpu.CompilerParams(vmem_limit_bytes=SMALL_VMEM),
    )(*routing, arrived, *entering)


def mixed_halves(tick, per_expert, slices, tables, back_ref, pairs):
    devices, block, half_width = back_ref.shape
    rows = devices * block
    back = back_ref[...].reshape(rows, half_width)
    terms = []
    for direction in range(2):
        _, weight = placing(
            tables[2 * direction], tables[2 * direction + 1], tick, direction, rows, per_expert, slices
        )
        side = half_of(rows, weight.shape[1], per_expert)
        sides = jnp.concatenate(
            [jnp.where(side == half, weight, 0.0) for half in range(2)], axis=1
        )
        high = sides.astype(jnp.bfloat16).astype(jnp.float32)
        middle = (sides - high).astype(jnp.bfloat16).astype(jnp.float32)
        terms += [sides - high - middle, middle, high]
    mixed = lax.dot_general(
        jnp.concatenate(terms, axis=1).astype(jnp.bfloat16),
        back,
        (((0,), (0,)), ((), ())),
        preferred_element_type=jnp.float32,
    )
    results = []
    for direction, halves in enumerate(pairs):
        total = jnp.concatenate([half.astype(jnp.float32) for half in halves], axis=0)
        count = total.shape[0]
        for term in range(3):
            start = (3 * direction + term) * count
            total = total + mixed[start : start + count]
        results.append(total.astype(jnp.bfloat16))
    return results


def relay_kernel(tick, per_expert, slices, *refs):
    tables, back_ref, token_refs, section_ref, next_refs = refs[:4], refs[4], refs[5:7], refs[7], refs[8:]
    half_width = back_ref.shape[2]
    section, last = lax.axis_index("section"), lax.axis_size("section") - 1
    pairs = [split_rows(tokens_ref[0]) for tokens_ref in token_refs]
    results = mixed_halves(tick, per_expert, slices, tables, back_ref, pairs)
    section_ref[...] = jnp.zeros_like(section_ref)
    for result, next_ref in zip(results, next_refs):
        count = result.shape[0] // 2
        for half in range(2):
            next_ref[:, half * half_width : (half + 1) * half_width] = result[
                half * count : (half + 1) * count
            ]

    @pl.when(section < last)
    def _():
        section_ref[jnp.minimum(section + 1, last)] = results[0]

    @pl.when(section > 0)
    def _():
        section_ref[jnp.maximum(section - 1, 0)] = results[1]


def relay(tick, per_expert, slices, routing, back, fwd, bwd):
    tokens, width = fwd.shape[-2:]
    sections = lax.axis_size("section")
    return pl.pallas_call(
        functools.partial(relay_kernel, tick, per_expert, slices),
        out_shape=[pltpu.VMEM((sections, 2 * tokens, width // 2), jnp.bfloat16)]
        + [pltpu.VMEM((tokens, width), jnp.bfloat16)] * 2,
        in_specs=[VMEM] * 7,
        out_specs=[VMEM] * 3,
        compiler_params=pltpu.CompilerParams(vmem_limit_bytes=SMALL_VMEM),
    )(*routing, back, fwd, bwd)


def finish_kernel(tick, per_expert, slices, *refs):
    tables, back_ref, section_ref, enter_refs, earlier_refs, out_refs = (
        refs[:4], refs[4], refs[5], refs[6:8], refs[8:10], refs[10:],
    )
    half_width = back_ref.shape[2]
    pairs = arriving(section_ref, enter_refs)
    results = mixed_halves(tick, per_expert, slices, tables, back_ref, pairs)
    for result, earlier_ref, out_ref in zip(results, earlier_refs, out_refs):
        count = result.shape[0] // 2
        out_ref[0, 0] = earlier_ref[...]
        for half in range(2):
            out_ref[tick, 0, :, half * half_width : (half + 1) * half_width] = result[
                half * count : (half + 1) * count
            ]


def finish(tick, per_expert, slices, routing, back, arrived, *others):
    tokens, width = others[0].shape
    return pl.pallas_call(
        functools.partial(finish_kernel, tick, per_expert, slices),
        out_shape=[jax.ShapeDtypeStruct((TICKS, 1, tokens, width), jnp.bfloat16)] * 2,
        in_specs=[VMEM] * 10,
        out_specs=[VMEM] * 2,
        compiler_params=pltpu.CompilerParams(vmem_limit_bytes=SMALL_VMEM),
    )(*routing, back, arrived, *others)


def home_of(line, slots, per_expert):
    half, direction, slot = line // (2 * slots), line // slots % 2, line % slots
    return (
        slot // per_expert * (4 * per_expert)
        + (2 * half + direction) * per_expert
        + slot % per_expert
    )


def expert_kernel(tick, rows_ref, saved_ref, w_in, w_out, out_ref):
    devices, block, half_width = rows_ref.shape
    per_expert = block // 4
    slots = devices * per_expert
    width, both = w_in.shape
    hidden_units = both // 2
    rows = devices * block

    received = rows_ref[...].reshape(rows, half_width)
    line = lax.broadcasted_iota(jnp.int32, (4 * slots, rows), 0)
    row = lax.broadcasted_iota(jnp.int32, (4 * slots, rows), 1)
    pick = jnp.where(row == home_of(line, slots, per_expert), 1.0, 0.0)
    picked = exact_dot(pick, received).astype(jnp.bfloat16)
    slot_rows = jnp.concatenate([picked[: 2 * slots], picked[2 * slots :]], axis=1)

    gate_up = jnp.dot(slot_rows[:slots], w_in[...], preferred_element_type=jnp.float32)
    grad = lax.dot_general(
        slot_rows[slots:],
        w_out[...],
        (((1,), (1,)), ((), ())),
        preferred_element_type=jnp.float32,
    )
    gate_pre = saved_ref[tick, 0, 0, :, :hidden_units]
    sigma = jax.nn.sigmoid(gate_pre)
    slope = sigma * (1.0 + gate_pre * (1.0 - sigma))
    joined_gate = (grad * saved_ref[tick, 0, 0, :, hidden_units:] * slope).astype(jnp.bfloat16)
    joined_up = (grad * (gate_pre * sigma)).astype(jnp.bfloat16)
    joined = jnp.concatenate([joined_gate, joined_up], axis=1)
    gate = gate_up[:, :hidden_units]
    hidden = (gate * jax.nn.sigmoid(gate) * gate_up[:, hidden_units:]).astype(jnp.bfloat16)
    back = lax.dot_general(
        joined, w_in[...], (((1,), (1,)), ((), ())), preferred_element_type=jnp.float32
    ).astype(jnp.bfloat16)
    ahead = jnp.dot(hidden, w_out[...], preferred_element_type=jnp.float32).astype(jnp.bfloat16)
    parts = jnp.concatenate(
        [ahead[:, :half_width], back[:, :half_width], ahead[:, half_width:], back[:, half_width:]],
        axis=0,
    )

    row = lax.broadcasted_iota(jnp.int32, (rows, 4 * slots), 0)
    line = lax.broadcasted_iota(jnp.int32, (rows, 4 * slots), 1)
    spread = jnp.where(row == home_of(line, slots, per_expert), 1.0, 0.0)
    out_ref[...] = exact_dot(spread, parts).astype(jnp.bfloat16).reshape(out_ref.shape)


def expert_step(tick, rows, saved_pre, w_in, w_out):
    width, both = w_in.shape
    slots = saved_pre.shape[3]
    return pl.pallas_call(
        functools.partial(expert_kernel, tick),
        out_shape=pltpu.VMEM(rows.shape, jnp.bfloat16),
        in_specs=[VMEM] * 4,
        out_specs=VMEM,
        compiler_params=pltpu.CompilerParams(vmem_limit_bytes=EXPERT_VMEM),
        cost_estimate=pl.CostEstimate(
            flops=12 * slots * width * (both // 2),
            bytes_accessed=0,
            transcendentals=0,
        ),
    )(rows, saved_pre, w_in, w_out)


def exchange(array, axis):
    return lax.all_to_all(array, axis, split_axis=0, concat_axis=0, tiled=True)


def shards(
    fwd_act,
    fwd_enter,
    bwd_grad,
    bwd_enter,
    w_in,
    w_out,
    fwd_route,
    fwd_gate,
    bwd_route,
    bwd_gate,
    saved_pre,
):
    devices = lax.axis_size("expert")
    slices = FF // w_out.shape[2]
    per_expert = saved_pre.shape[3] // devices
    routing = [
        jnp.swapaxes(table, 2, 3) for table in (fwd_route, fwd_gate, bwd_route, bwd_gate)
    ]
    beside = BESIDE * (w_in.size + w_out.size)
    w_in, w_out = (
        pltpu.with_memory_space_constraint(w.reshape(w.shape[2:]), pltpu.VMEM) for w in (w_in, w_out)
    )
    saved_pre = pltpu.with_memory_space_constraint(saved_pre, pltpu.VMEM)
    sent = first_pack(0, devices, per_expert, slices, routing, fwd_act, bwd_grad, beside)
    parts = expert_step(0, exchange(sent, "expert"), saved_pre, w_in, w_out)
    moved, fwd_next, bwd_next = relay(
        0, per_expert, slices, routing, exchange(parts, "expert"), fwd_act, bwd_grad
    )
    arrived = exchange(moved, "section")
    sent = later_pack(1, devices, per_expert, slices, routing, arrived, fwd_enter, bwd_enter)
    parts = expert_step(1, exchange(sent, "expert"), saved_pre, w_in, w_out)
    return finish(
        1, per_expert, slices, routing, exchange(parts, "expert"), arrived,
        fwd_enter, bwd_enter, fwd_next, bwd_next,
    )


def solution(mesh):
    placed = (
        P("section", "expert", None),
        P("expert", None),
        P("section", "expert", None),
        P("expert", None),
        P("section", "expert", None, None),
        P("section", "expert", None, None),
        P(None, "section", "expert", None),
        P(None, "section", "expert", None),
        P(None, "section", "expert", None),
        P(None, "section", "expert", None),
        P(None, "section", "expert", None, None),
    )
    return jax.shard_map(
        shards,
        mesh=mesh,
        in_specs=placed,
        out_specs=(P(None, "section", "expert", None), P(None, "section", "expert", None)),
        check_vma=False,
    )
```
